256 devices in a mesh: dp: 8 (over x, core), tile: 32 (over z, y).
Axes of the slice: x: 4, y: 4, z: 8, core: 2. Of those that a mesh axis runs over, the one named last changes fastest.
Arguments:
- acts: bfloat16 [3840, 12, 4096], P(('dp', 'tile')), may hold values from -40 to 40
- grads: bfloat16 [3840, 12, 4096], P(('dp', 'tile')), may hold values from -40 to 40
- lengths: int32 [3840], P(('dp', 'tile')), may hold values from 0 to 12, as said below
- assign: int32 [3840], P(('dp', 'tile')), may hold values from -1 to 95, as said below
Outputs:
- act_factor: float32 [4096, 4096], P('tile', 'dp')
- grad_factor: float32 [4096, 4096], P('tile', 'dp')
- block_norms: float32 [3072], P(('dp', 'tile'))
The draws below stay inside these ranges and needn't reach their ends.
Inputs may be any that keep to these rules, and one draw needn't show every extreme that they name: `lengths`: 0 exactly for an empty slot; a live block holds 1 to 12 tokens, its first ones; in each index of tile exactly 96 of the 120 slots are live, and one device of it has all 15 slots live. `assign`: -1 exactly for empty slots; within one index of tile the live blocks take each value 0 to 95 once; value q names index of dp q // 12, and the blocks of one device name one index of dp at most 2 times.
All inputs are finite; a program needn't handle non-finite values.
Results may differ from the reference program's by a relative error of at most 0.0003.
Values may be sent and summed in bfloat16 or wider, within the bound.
No kernel may reach another device: no remote copies, remote signals or barrier semaphores. Data moves between devices by JAX's collectives and lax.ppermute only.
A program may use at most 128 MiB of HBM per device.

```python
import math
import jax
import jax.numpy as jnp
from jax import lax

W = 4096
BLOCK = 12
KEEP = 12
SLOTS = 15
BLOCKS = 3840
N_DP = 8
N_TILE = 32


def layout_plan(key):
    slot_total = N_DP * SLOTS

    def column(tile_index):
        column_key = jax.random.fold_in(key, tile_index)
        keys = jax.random.split(column_key, 5)
        full_source = jax.random.randint(keys[0], (), 0, N_DP)
        positions = jnp.arange(slot_total, dtype=jnp.int32)
        source = positions // SLOTS
        shuffled = jax.random.permutation(keys[1], slot_total).astype(jnp.int32)
        ranking_score = jnp.where(source == full_source, positions - slot_total, shuffled)
        ordering = jnp.argsort(ranking_score, stable=True)
        is_live = jnp.zeros((slot_total,), jnp.int32).at[ordering[:N_DP * KEEP]].set(1)
        live_rank = jnp.cumsum(is_live) - 1
        target_dp = jnp.mod(live_rank, N_DP)
        within = jnp.clip(live_rank // N_DP, 0, KEEP - 1)

        def shuffle_keep(sub_key):
            return jax.random.permutation(sub_key, KEEP).astype(jnp.int32)
        slot_perm = jax.vmap(shuffle_keep)(jax.random.split(keys[2], N_DP))
        target_slot = slot_perm[target_dp, within]
        placing = jnp.where(is_live == 1, target_dp * KEEP + target_slot, -1)
        full_coin = jax.random.randint(keys[3], (slot_total,), 0, 8)
        short_len = jax.random.randint(keys[4], (slot_total,), 1, BLOCK + 1)
        forced = positions == full_source * SLOTS
        length = jnp.where(is_live == 1, jnp.where((full_coin >= 1) | forced, BLOCK, short_len), 0)
        return (length.reshape(N_DP, SLOTS), placing.reshape(N_DP, SLOTS))
    lengths, placing = jax.vmap(column)(jnp.arange(N_TILE, dtype=jnp.int32))
    lengths = lengths.transpose(1, 0, 2).reshape(-1).astype(jnp.int32)
    placing = placing.transpose(1, 0, 2).reshape(-1).astype(jnp.int32)
    return (lengths, placing)


def draw_lengths(key, part):
    lengths, placing = layout_plan(key)
    return lengths


def draw_assign(key, part):
    lengths, placing = layout_plan(key)
    return placing


def draw_acts(key, part):
    key = jax.random.fold_in(key, 11)
    keys = jax.random.split(key, 3)
    full_shape = (BLOCKS, BLOCK, W)
    col_scale = jnp.exp(jax.random.uniform(keys[0], (W,), jnp.float32, math.log(0.3), math.log(3.0)))
    row_scale = jnp.exp(jax.random.uniform(keys[1], (BLOCKS, BLOCK, 1), jnp.float32, math.log(0.3), math.log(3.0)))
    base = jnp.clip(jax.random.normal(keys[2], full_shape, jnp.float32), -4.0, 4.0)
    return (base * row_scale * col_scale).astype(jnp.bfloat16)


def draw_grads(key, part):
    key = jax.random.fold_in(key, 12)
    keys = jax.random.split(key, 3)
    full_shape = (BLOCKS, BLOCK, W)
    col_scale = jnp.exp(jax.random.uniform(keys[0], (W,), jnp.float32, math.log(0.3), math.log(3.0)))
    row_scale = jnp.exp(jax.random.uniform(keys[1], (BLOCKS, BLOCK, 1), jnp.float32, math.log(0.3), math.log(3.0)))
    base = jnp.clip(jax.random.normal(keys[2], full_shape, jnp.float32), -4.0, 4.0)
    return (base * row_scale * col_scale).astype(jnp.bfloat16)


def setup_inputs(seed: int = 0) -> dict:
    key_of = jax.random.split(jax.random.key(seed), 5)
    return {
        "acts": draw_acts(jax.random.fold_in(key_of[4], 71), 0),
        "grads": draw_grads(jax.random.fold_in(key_of[4], 71), 0),
        "lengths": draw_lengths(jax.random.fold_in(key_of[4], 71), 0),
        "assign": draw_assign(jax.random.fold_in(key_of[4], 71), 0),
    }


def reference(acts, grads, lengths, assign):
    places = N_DP * KEEP
    act_view = acts.reshape(N_DP, N_TILE, SLOTS, BLOCK, W)
    grad_view = grads.reshape(N_DP, N_TILE, SLOTS, BLOCK, W)
    len_view = lengths.reshape(N_DP, N_TILE, SLOTS)
    target_view = assign.reshape(N_DP, N_TILE, SLOTS)
    positions = jnp.arange(BLOCK, dtype=jnp.int32)

    def column(running, tile_index):
        group_acts = lax.dynamic_index_in_dim(act_view, tile_index, 1, keepdims=False).reshape(N_DP * SLOTS, BLOCK, W)
        group_grads = lax.dynamic_index_in_dim(grad_view, tile_index, 1, keepdims=False).reshape(N_DP * SLOTS, BLOCK, W)
        group_lens = lax.dynamic_index_in_dim(len_view, tile_index, 1, keepdims=False).reshape(-1)
        targets = lax.dynamic_index_in_dim(target_view, tile_index, 1, keepdims=False).reshape(-1)
        live_tokens = (positions[None, :] < group_lens[:, None]).astype(acts.dtype)[:, :, None]
        masked_acts = group_acts * live_tokens
        masked_grads = group_grads * live_tokens
        wide_acts = masked_acts.astype(jnp.float32)
        wide_grads = masked_grads.astype(jnp.float32)
        self_acts = jnp.einsum('btw,bsw->bts', wide_acts, wide_acts, precision=lax.Precision.HIGHEST)
        self_grads = jnp.einsum('btw,bsw->bts', wide_grads, wide_grads, precision=lax.Precision.HIGHEST)
        scores = jnp.sum(self_acts * self_grads, axis=(1, 2)) * (1.0 / (W * W * BLOCK))
        where_to = jnp.where(targets >= 0, targets, places).astype(jnp.int32)
        kept_acts = jnp.zeros((places, BLOCK, W), acts.dtype).at[where_to].set(masked_acts, mode="drop")
        kept_grads = jnp.zeros((places, BLOCK, W), grads.dtype).at[where_to].set(masked_grads, mode="drop")
        placed = jnp.zeros((places,), jnp.float32).at[where_to].set(scores, mode="drop")
        rows_acts = kept_acts.reshape(places * BLOCK, W)
        rows_grads = kept_grads.reshape(places * BLOCK, W)
        partial_acts = jnp.dot(rows_acts.T, rows_acts, preferred_element_type=jnp.float32)
        partial_grads = jnp.dot(rows_grads.T, rows_grads, preferred_element_type=jnp.float32)
        running = (running[0] + partial_acts, running[1] + partial_grads)
        return running, placed

    zeros_square = jnp.zeros((W, W), jnp.float32)
    sums, placed_all = lax.scan(column, (zeros_square, zeros_square), jnp.arange(N_TILE, dtype=jnp.int32))
    scale = 1.0 / (N_DP * N_TILE * KEEP * BLOCK)
    block_norms = placed_all.reshape(N_TILE, N_DP, KEEP).transpose(1, 0, 2).reshape(-1)
    return sums[0] * scale, sums[1] * scale, block_norms
```

```python
import jax
import jax.numpy as jnp
from jax import lax
from jax.sharding import PartitionSpec as P

KEEP = 12
NX, NK, NZ, NY = 4, 2, 8, 4
AXES = ("dp", "tile")


def route(x=0, k=0, z=0, y=0, swap=False):
    pairs = []
    for sx in range(NX):
        for sk in range(NK):
            for sz in range(NZ):
                for sy in range(NY):
                    tx, tk, tz, ty = (sx + x) % NX, (sk + k) % NK, (sz + z) % NZ, (sy + y) % NY
                    if swap:
                        tx, ty = ty, tx
                    source = ((sx * NK + sk) * NZ + sz) * NY + sy
                    pairs.append((source, ((tx * NK + tk) * NZ + tz) * NY + ty))
    return pairs


def send(value, **shift):
    return lax.ppermute(value, AXES, route(**shift))


def inner_rows(left_part, right_part):
    return lax.dot_general(
        left_part, right_part, (((0,), (0,)), ((), ())), preferred_element_type=jnp.float32
    )


def score_blocks(data_acts, data_grads):
    block_len = data_acts.shape[1]
    feat_width = data_acts.shape[2]
    self_acts = jnp.einsum("btw,bsw->bts", data_acts, data_acts, preferred_element_type=jnp.float32)
    self_grads = jnp.einsum(
        "btw,bsw->bts", data_grads, data_grads, preferred_element_type=jnp.float32
    )
    return jnp.sum(self_acts * self_grads, axis=(1, 2)) * (
        1.0 / (feat_width * feat_width * block_len)
    )


def gather_line(flat, axis):
    first, second = flat[:96], flat[96:]
    up, down = {axis: 1}, {axis: -1}
    up_first, down_second = send(first, **up), send(second, **down)
    up_second, down_first = send(second, **up), send(first, **down)
    far_first, far_second = send(up_first, **up), send(down_second, **down)
    near = [flat, up_first, up_second, down_first, down_second]
    near = near + [send(part, k=1) for part in near]
    far = [far_first, far_second]
    far = far + [send(part, k=1) for part in far]
    return near, far


def partial_factor(near, far, place, span):
    near, far = jnp.concatenate(near, axis=0), jnp.concatenate(far, axis=0)
    early = inner_rows(near, lax.dynamic_slice_in_dim(near, place * span, span, 1))
    return early + inner_rows(far, lax.dynamic_slice_in_dim(far, place * span, span, 1))


def reduce_line(partial, axis, me, scale):
    half = NZ // 2
    up, down = {axis: 1}, {axis: -1}

    def part(step):
        return lax.dynamic_index_in_dim(partial, jnp.mod(me + step, 4), 1, keepdims=False) * scale

    def narrow(value):
        return value.astype(jnp.float16)

    far, right, left, mine = part(2), part(1), part(3), part(0)
    relay_up = send(narrow(far[:half]), **up)
    relay_down = send(narrow(far[half:]), **down)
    plain_up = send(narrow(right[half:]), **up)
    plain_down = send(narrow(left[:half]), **down)
    last_up = send(narrow(right[:half] + relay_up.astype(jnp.float32)), **up)
    last_down = send(narrow(left[half:] + relay_down.astype(jnp.float32)), **down)
    low = mine[:half] + last_up.astype(jnp.float32) + plain_down.astype(jnp.float32)
    high = mine[half:] + last_down.astype(jnp.float32) + plain_up.astype(jnp.float32)
    return jnp.concatenate([low, high], axis=0)


def reduce_z(value, me):
    half = value.shape[1] // 2

    def part(step):
        return lax.dynamic_index_in_dim(value, jnp.mod(me + step, NZ), 0, keepdims=False)

    far = part(4)
    up, down = send(far[:half], z=1), send(far[half:], z=-1)
    near_up, near_down = part(3), part(-3)
    up = send(jnp.concatenate([near_up[:half] + up, near_up[half:]], axis=0), z=1)
    down = send(jnp.concatenate([near_down[:half], near_down[half:] + down], axis=0), z=-1)
    up, down = send(part(2) + up, z=1), send(part(-2) + down, z=-1)
    up, down = send(part(1) + up, z=1), send(part(-1) + down, z=-1)
    return part(0) + up + down


def body(acts, grads, lengths, assign):
    n_dp = lax.axis_size("dp")
    n_tile = lax.axis_size("tile")
    slot_count, block_len, feat_width = acts.shape
    span = feat_width // n_dp
    dp, tile = lax.axis_index("dp"), lax.axis_index("tile")
    my_x, my_k = dp // NK, dp % NK
    my_z, my_y = tile // NY, tile % NY
    positions = jnp.arange(block_len, dtype=jnp.int32)
    live_tokens = (positions[None, :] < lengths[:, None]).astype(jnp.bfloat16)[:, :, None]
    masked_acts = acts * live_tokens
    masked_grads = grads * live_tokens

    near_a, far_a = gather_line(masked_acts.reshape(-1, feat_width), "x")
    near_g, far_g = gather_line(masked_grads.reshape(-1, feat_width), "y")

    scores = score_blocks(masked_acts, masked_grads)
    places = jnp.arange(n_dp * KEEP, dtype=jnp.int32)
    placed = jnp.sum(jnp.where(assign[:, None] == places[None, :], scores[:, None], 0.0), axis=0)
    got = lax.all_to_all(placed.reshape(n_dp, KEEP), "dp", split_axis=0, concat_axis=0, tiled=True)
    block_norms = jnp.sum(got, axis=0)

    peaks = jnp.stack([jnp.max(jnp.abs(v)).astype(jnp.float32) for v in (masked_acts, masked_grads)])
    peaks = lax.pmax(peaks, AXES)
    narrowing = 30000.0 / (2 * n_dp * slot_count * block_len * jnp.maximum(peaks * peaks, 1e-35))

    shape = (NZ, NY, feat_width // n_tile, span)
    part_a = partial_factor(near_a, far_a, 2 * my_x + my_k, span).reshape(shape)
    part_g = partial_factor(near_g, far_g, 2 * my_y + my_k, span).reshape(shape)
    line_a = reduce_line(part_a, "y", my_y, narrowing[0])
    line_g = reduce_line(part_g, "x", my_x, narrowing[1])
    scale = 1.0 / (n_dp * n_tile * KEEP * block_len)
    act_factor = reduce_z(line_a, my_z) * (scale / narrowing[0])
    grad_factor = send(reduce_z(line_g, my_z) * (scale / narrowing[1]), swap=True)
    return (act_factor, grad_factor, block_norms)


def solution(mesh):
    in_specs = (
        P(("dp", "tile"), None, None),
        P(("dp", "tile"), None, None),
        P(("dp", "tile")),
        P(("dp", "tile")),
    )
    out_specs = (P("tile", "dp"), P("tile", "dp"), P(("dp", "tile")))
    return jax.shard_map(body, mesh=mesh, in_specs=in_specs, out_specs=out_specs, check_vma=False)
```

```python
import functools

import jax
import jax.numpy as jnp
from jax import lax
from jax.experimental import pallas as pl
from jax.experimental.pallas import tpu as pltpu
from jax.sharding import PartitionSpec as P

KEEP = 12
NX, NK, NZ, NY = 4, 2, 8, 4
AXES = ("dp", "tile")
VMEM_BYTES = 56 * 1024 * 1024


def route(x=0, k=0, z=0, y=0):
    pairs = []
    for sx in range(NX):
        for sk in range(NK):
            for sz in range(NZ):
                for sy in range(NY):
                    tx, tk, tz, ty = (sx + x) % NX, (sk + k) % NK, (sz + z) % NZ, (sy + y) % NY
                    source = ((sx * NK + sk) * NZ + sz) * NY + sy
                    pairs.append((source, ((tx * NK + tk) * NZ + tz) * NY + ty))
    return pairs


def send(value, **shift):
    return lax.ppermute(value, AXES, route(**shift))


def token_rows(tokens, live):
    slots, count, width = tokens.shape
    by_position = jnp.pad(jnp.transpose(tokens, (1, 0, 2)), ((0, 0), (0, 16 - slots), (0, 0)))
    return jnp.where(live, by_position, 0).reshape(count * 16, width)


def block_scores(rows_a, rows_g, count):
    def gram(rows):
        return lax.dot_general(
            rows, rows, (((1,), (1,)), ((), ())), preferred_element_type=jnp.float32
        )

    slot = jnp.arange(rows_a.shape[0], dtype=jnp.int32) % 16
    same = slot[:, None] == slot[None, :]
    per_row = jnp.sum(jnp.where(same, gram(rows_a) * gram(rows_g), 0.0), axis=1)
    width = rows_a.shape[1]
    return jnp.sum(per_row.reshape(count, 16), axis=0) * (1.0 / (width * width * count))


def load(pieces, buf, sems):
    copies, start = [], 0
    for i, piece in enumerate(pieces):
        copies.append(pltpu.make_async_copy(piece, buf.at[pl.ds(start, piece.shape[0])], sems.at[i]))
        start += piece.shape[0]
    for copy in copies:
        copy.start()
    for copy in copies:
        copy.wait()


def largest(buf):
    def step(i, so_far):
        return jnp.maximum(so_far, jnp.abs(buf[pl.ds(pl.multiple_of(i * 16, 16), 16), :]))

    zeros = jnp.zeros((16, buf.shape[1]), buf.dtype)
    return jnp.max(lax.fori_loop(0, buf.shape[0] // 16, step, zeros).astype(jnp.float32))


def turn_columns(place, buf, left):
    left[...] = jnp.transpose(buf[:, pl.ds(pl.multiple_of(place * 512, 512), 512)])


def turn_quarter(place, buf, left):
    for z in range(NZ):
        at = pl.multiple_of(z * 512 + place * 128, 128)
        left[z * 128 : (z + 1) * 128, :] = jnp.transpose(buf[:, pl.ds(at, 128)])


def times_columns(buf, left, place):
    return jnp.dot(
        left[...],
        buf[:, pl.ds(pl.multiple_of(place * 512, 512), 512)],
        preferred_element_type=jnp.float32,
    )


def act_near_kernel(at, *refs, count):
    pieces, (out, peak, buf, left, sems) = refs[:count], refs[count:]

    @pl.when(pl.program_id(0) == 0)
    def _():
        load(pieces, buf, sems)
        turn_columns(at[0], buf, left)
        peak[...] = jnp.full(peak.shape, largest(buf), jnp.float32)

    out[...] = times_columns(buf, left, pl.program_id(0))


def act_far_kernel(at, near_peak, near, *refs, count):
    pieces, (out, peak, buf, left, sems) = refs[:count], refs[count:]

    @pl.when(pl.program_id(0) == 0)
    def _():
        load(pieces, buf, sems)
        turn_columns(at[0], buf, left)
        peak[...] = jnp.maximum(near_peak[...], largest(buf))

    total = near[...] + times_columns(buf, left, pl.program_id(0))
    for quarter in range(4):
        out[lax.rem(quarter - at[1] + 4, 4), 0] = total[:, quarter * 128 : (quarter + 1) * 128]


def grad_near_kernel(at, *refs, count):
    pieces, (out, peak, buf, left, sems) = refs[:count], refs[count:]

    @pl.when(pl.program_id(0) == 0)
    def _():
        load(pieces, buf, sems)
        turn_quarter(at[0], buf, left)
        peak[...] = jnp.full(peak.shape, largest(buf), jnp.float32)

    target = lax.rem(at[2] + pl.program_id(0), 4)
    out[0] = times_columns(buf, left, 2 * target + at[1])


def grad_far_kernel(at, near_peak, near, *refs, count):
    pieces, (out, peak, buf, left, sems) = refs[:count], refs[count:]

    @pl.when(pl.program_id(0) == 0)
    def _():
        load(pieces, buf, sems)
        turn_quarter(at[0], buf, left)
        peak[...] = jnp.maximum(near_peak[...], largest(buf))

    target = lax.rem(at[2] + pl.program_id(0), 4)
    total = near[0] + times_columns(buf, left, 2 * target + at[1])
    for z in range(NZ):
        out[0, lax.rem(z - at[3] + NZ, NZ)] = total[z * 128 : (z + 1) * 128]


def product(kernel, at, pieces, steps, left_rows, before, before_specs, out_shape, out_spec):
    count, rows, width = len(pieces), sum(p.shape[0] for p in pieces), pieces[0].shape[1]
    peak_spec = pl.BlockSpec((8, 128), lambda i, at: (0, 0))
    return pl.pallas_call(
        functools.partial(kernel, count=count),
        grid_spec=pltpu.PrefetchScalarGridSpec(
            num_scalar_prefetch=1,
            grid=(steps,),
            in_specs=[peak_spec] * (len(before) > 0)
            + before_specs
            + [pl.BlockSpec(memory_space=pl.ANY)] * count,
            out_specs=[out_spec, peak_spec],
            scratch_shapes=[
                pltpu.VMEM((rows, width), jnp.bfloat16),
                pltpu.VMEM((left_rows, rows), jnp.bfloat16),
                pltpu.SemaphoreType.DMA((count,)),
            ],
        ),
        out_shape=[
            jax.ShapeDtypeStruct(out_shape, jnp.float32),
            jax.ShapeDtypeStruct((8, 128), jnp.float32),
        ],
        compiler_params=pltpu.CompilerParams(vmem_limit_bytes=VMEM_BYTES),
        cost_estimate=pl.CostEstimate(
            flops=2 * rows * 512 * width, bytes_accessed=2 * rows * width + 8 * 512 * width, transcendentals=0
        ),
    )(jnp.stack(at), *before, *pieces)


def act_partial(near, far, at):
    out_spec = pl.BlockSpec((512, 512), lambda i, at: (0, i))
    out, peak = product(act_near_kernel, at, near, 8, 512, [], [], (512, 4096), out_spec)
    spec = pl.BlockSpec((4, 1, 512, 128), lambda i, at: (0, lax.rem(i - at[2] + NZ, NZ), 0, 0))
    return product(
        act_far_kernel, at, far, 8, 512, [peak, out], [out_spec], (4, NZ, 512, 128), spec
    )


def grad_partial(near, far, at):
    out_spec = pl.BlockSpec((1, 1024, 512), lambda i, at: (i, 0, 0))
    out, peak = product(grad_near_kernel, at, near, 4, 1024, [], [], (4, 1024, 512), out_spec)
    spec = pl.BlockSpec((1, NZ, 128, 512), lambda i, at: (i, 0, 0, 0))
    return product(
        grad_far_kernel, at, far, 4, 1024, [peak, out], [out_spec], (4, NZ, 128, 512), spec
    )


def gather_line(rows, axis):
    up, down = {axis: 1}, {axis: -1}
    half = rows.shape[0] // 2
    below, above = send(rows, **up), send(rows, **down)
    far = [send(below[:half], **up), send(above[half:], **down)]
    near = [rows, below, above]
    return near + [send(part, k=1) for part in near], far + [send(part, k=1) for part in far]


def reduce_line(partial, peak, tokens, axis, factor):
    half = NZ // 2
    up, down = {axis: 1}, {axis: -1}
    bound = peak * peak
    for other in [send(peak, **{axis: step}) for step in (1, 2, 3)]:
        bound = jnp.maximum(bound, other * other)
    scale = (30000.0 / (2 * tokens * jnp.maximum(bound, 1e-35)))[0, 0]

    def narrow(value):
        return value.astype(jnp.float16)

    def widen(value):
        return value.astype(jnp.float32)

    mine, right, far, left = partial[0] * scale, partial[1] * scale, partial[2] * scale, partial[3] * scale
    relay_up = send(narrow(far[:half]), **up)
    relay_down = send(narrow(far[half:]), **down)
    plain_up = send(narrow(right[half:]), **up)
    plain_down = send(narrow(left[:half]), **down)
    last_up = send(narrow(right[:half] + widen(relay_up)), **up)
    last_down = send(narrow(left[half:] + widen(relay_down)), **down)
    low = mine[:half] + widen(last_up) + widen(plain_down)
    high = mine[half:] + widen(last_down) + widen(plain_up)
    return jnp.concatenate([low, high], axis=0) * (factor / scale)


def reduce_z(value):
    half = value.shape[1] // 2
    up, down = send(value[4, :half], z=1), send(value[4, half:], z=-1)
    up = send(jnp.concatenate([value[3, :half] + up, value[3, half:]], axis=0), z=1)
    down = send(jnp.concatenate([value[5, :half], value[5, half:] + down], axis=0), z=-1)
    up, down = send(value[2] + up, z=1), send(value[6] + down, z=-1)
    up, down = send(value[1] + up, z=1), send(value[7] + down, z=-1)
    return value[0] + up + down


def body(acts, grads, lengths, assign):
    n_dp = lax.axis_size("dp")
    n_tile = lax.axis_size("tile")
    slot_count, block_len, feat_width = acts.shape
    dp, tile = lax.axis_index("dp"), lax.axis_index("tile")
    my_x, my_k = dp // NK, dp % NK
    my_z, my_y = tile // NY, tile % NY
    positions = jnp.arange(block_len, dtype=jnp.int32)
    live = (positions[:, None] < jnp.pad(lengths, (0, 16 - slot_count))[None, :])[:, :, None]
    rows_a, rows_g = token_rows(acts, live), token_rows(grads, live)

    near_a, far_a = gather_line(rows_a, "x")
    near_g, far_g = gather_line(rows_g, "y")

    scores = block_scores(rows_a, rows_g, block_len)[:slot_count]
    places = jnp.arange(n_dp * KEEP, dtype=jnp.int32)
    placed = jnp.sum(jnp.where(assign[:, None] == places[None, :], scores[:, None], 0.0), axis=0)
    got = lax.all_to_all(placed.reshape(n_dp, KEEP), "dp", split_axis=0, concat_axis=0, tiled=True)
    block_norms = jnp.sum(got, axis=0)

    part_a, peak_a = act_partial(near_a, far_a, [2 * my_x + my_k, my_y, my_z])
    part_g, peak_g = grad_partial(near_g, far_g, [my_y, my_k, my_x, my_z])
    tokens = n_dp * slot_count * block_len
    factor = 1.0 / (n_dp * n_tile * KEEP * block_len)
    act_factor = jnp.transpose(reduce_z(reduce_line(part_a, peak_a, tokens, "y", factor)))
    grad_factor = reduce_z(reduce_line(part_g, peak_g, tokens, "x", factor))
    return (act_factor, grad_factor, block_norms)


def solution(mesh):
    in_specs = (
        P(("dp", "tile"), None, None),
        P(("dp", "tile"), None, None),
        P(("dp", "tile")),
        P(("dp", "tile")),
    )
    out_specs = (P("tile", "dp"), P("tile", "dp"), P(("dp", "tile")))
    return jax.shard_map(body, mesh=mesh, in_specs=in_specs, out_specs=out_specs, check_vma=False)
```

```python
import functools

import jax
import jax.numpy as jnp
from jax import lax
from jax.experimental import pallas as pl
from jax.experimental.pallas import tpu as pltpu
from jax.sharding import PartitionSpec as P

KEEP = 12
NX, NK, NZ, NY = 4, 2, 8, 4
AXES = ("dp", "tile")
VMEM_BYTES = 26 * 1024 * 1024


def route(x=0, k=0, z=0, y=0, fan=None):
    pairs = []
    for sx in range(NX):
        for sk in range(NK):
            for sz in range(NZ):
                for sy in range(NY):
                    step = 1 - 2 * sk
                    tx = (sx + x + step * (fan == "x")) % NX
                    ty = (sy + y + step * (fan == "y")) % NY
                    tk, tz = (sk + k) % NK, (sz + z) % NZ
                    source = ((sx * NK + sk) * NZ + sz) * NY + sy
                    pairs.append((source, ((tx * NK + tk) * NZ + tz) * NY + ty))
    return pairs


def send(value, **shift):
    return lax.ppermute(value, AXES, route(**shift))


def token_rows(tokens, live):
    slots, count, width = tokens.shape
    by_position = jnp.pad(jnp.transpose(tokens, (1, 0, 2)), ((0, 0), (0, 16 - slots), (0, 0)))
    return jnp.where(live, by_position, 0).reshape(count * 16, width)


def block_scores(rows_a, rows_g, count):
    def gram(rows):
        return lax.dot_general(
            rows, rows, (((1,), (1,)), ((), ())), preferred_element_type=jnp.float32
        )

    slot = jnp.arange(rows_a.shape[0], dtype=jnp.int32) % 16
    same = slot[:, None] == slot[None, :]
    per_row = jnp.sum(jnp.where(same, gram(rows_a) * gram(rows_g), 0.0), axis=1)
    width = rows_a.shape[1]
    return jnp.sum(per_row.reshape(count, 16), axis=0) * (1.0 / (width * width * count))


def load(pieces, buf, sems):
    copies, start = [], 0
    for i, piece in enumerate(pieces):
        copies.append(pltpu.make_async_copy(piece, buf.at[pl.ds(start, piece.shape[0])], sems.at[i]))
        start += piece.shape[0]
    for copy in copies:
        copy.start()
    for copy in copies:
        copy.wait()


def largest(buf):
    def step(i, so_far):
        return jnp.maximum(so_far, jnp.abs(buf[pl.ds(pl.multiple_of(i * 16, 16), 16), :]))

    zeros = jnp.zeros((16, buf.shape[1]), buf.dtype)
    return jnp.max(lax.fori_loop(0, buf.shape[0] // 16, step, zeros).astype(jnp.float32))


def lanes(place):
    return pl.ds(pl.multiple_of(place * 128, 128), 128)


def load_and_turn(acts, at, pieces, buf, left, picked, sems):
    load(pieces, buf, sems)
    if acts:
        left[...] = jnp.transpose(buf[:, pl.ds(pl.multiple_of(at[0] * 1024, 1024), 1024)])
        for role in range(4):
            for i in range(4):
                unit = (role * 4 + i) * 128
                picked[:, unit : unit + 128] = buf[:, lanes(unit_tile(role, i, at))]
    else:
        for z in range(NZ):
            left[z * 128 : (z + 1) * 128, :] = jnp.transpose(buf[:, lanes(lax.rem(z + at[2], NZ) * 4 + at[0])])


def target_of(role, at):
    ahead = jnp.where(at[3] == 0, 1, 3)
    away = jnp.where(role == 0, 2, jnp.where(role == 3, 0, ahead))
    return lax.rem(at[1] + away, 4)


def half_of(role, at):
    return jnp.where(role == 1, 1 - at[3], at[3])


def unit_tile(role, i, at):
    z = lax.rem(half_of(role, at) * 4 + i + at[2], NZ)
    return z * 4 + target_of(role, at)


def products(acts, at, buf, left, picked, store):
    role = pl.program_id(0)
    if acts:
        columns = picked[:, pl.ds(pl.multiple_of(role * 512, 512), 512)]
        out = jnp.dot(left[...], columns, preferred_element_type=jnp.float32)
        for i in range(4):
            store(i, slice(0, 1024), out[:, i * 128 : (i + 1) * 128])
        return
    rows = left[pl.ds(pl.multiple_of(half_of(role, at) * 512, 512), 512), :]
    for core in range(2):
        start = pl.multiple_of((2 * target_of(role, at) + core) * 512, 512)
        out = jnp.dot(rows, buf[:, pl.ds(start, 512)], preferred_element_type=jnp.float32)
        for i in range(4):
            for part in range(4):
                tile = out[i * 128 : (i + 1) * 128, part * 128 : (part + 1) * 128]
                store(i, slice((core * 4 + part) * 128, (core * 4 + part + 1) * 128), tile)


def early_kernel(at, *refs, count, acts):
    pieces, (out, peak, buf, left, picked, sems) = refs[:count], refs[count:]

    @pl.when(pl.program_id(0) == 0)
    def _():
        load_and_turn(acts, at, pieces, buf, left, picked, sems)
        peak[...] = jnp.full(peak.shape, largest(buf), jnp.float32)

    def store(i, rows, value):
        out[0, i, rows] = value

    products(acts, at, buf, left, picked, store)


def late_kernel(at, early_peak, early, *refs, count, acts, tokens):
    pieces, (sent, kept, buf, left, picked, exponent, sems) = refs[:count], refs[count:]

    @pl.when(pl.program_id(0) == 0)
    def _():
        load_and_turn(acts, at, pieces, buf, left, picked, sems)
        peak = jnp.maximum(early_peak[0:1, :], largest(buf))
        bound = tokens * jnp.maximum(peak * peak, 1e-35)
        exponent[...] = jnp.broadcast_to(jnp.floor(jnp.log2(30000.0 / bound)), exponent.shape)

    def into(out, scale):
        def store(i, rows, value):
            out[0, i, rows] = (early[0, i, rows] + value) * scale

        products(acts, at, buf, left, picked, store)
        for i in range(4):
            out[0, i, 1024:1040] = exponent[...]

    @pl.when(pl.program_id(0) < 2)
    def _():
        into(sent, jnp.exp2(exponent[0:1, :]))

    @pl.when(pl.program_id(0) >= 2)
    def _():
        into(kept, 1.0)


def product(acts, at, pieces, early=(), tokens=None):
    count, rows, width = len(pieces), sum(p.shape[0] for p in pieces), pieces[0].shape[1]
    peak_spec = pl.BlockSpec((8, 128), lambda i, at: (0, 0))
    peak_shape = jax.ShapeDtypeStruct((8, 128), jnp.float32)
    spec = pl.BlockSpec((1, 4, 1024, 128), lambda i, at: (i, 0, 0, 0))
    scratch = [
        pltpu.VMEM((rows, width), jnp.bfloat16),
        pltpu.VMEM((1024, rows), jnp.bfloat16),
        pltpu.VMEM((rows, 2048) if acts else (16, 128), jnp.bfloat16),
    ]
    if early:
        kernel = functools.partial(late_kernel, tokens=tokens)
        before = [peak_spec, spec]
        out_specs = [
            pl.BlockSpec((1, 4, 1040, 128), lambda i, at: (jnp.minimum(i, 1), 0, 0, 0)),
            pl.BlockSpec((1, 4, 1040, 128), lambda i, at: (jnp.maximum(i - 2, 0), 0, 0, 0)),
        ]
        out_shape = [jax.ShapeDtypeStruct((2, 4, 1040, 128), jnp.float32)] * 2
        scratch.append(pltpu.VMEM((16, 128), jnp.float32))
        cost = pl.CostEstimate(
            flops=2 * rows * 1024 * 2048, bytes_accessed=2 * rows * width + 2 * 2048 * 4096, transcendentals=0
        )
    else:
        kernel, before = early_kernel, []
        out_specs = [spec, peak_spec]
        out_shape = [jax.ShapeDtypeStruct((4, 4, 1024, 128), jnp.float32), peak_shape]
        cost = pl.CostEstimate(flops=1, bytes_accessed=1, transcendentals=0)
    return pl.pallas_call(
        functools.partial(kernel, count=count, acts=acts),
        grid_spec=pltpu.PrefetchScalarGridSpec(
            num_scalar_prefetch=1,
            grid=(4,),
            in_specs=before + [pl.BlockSpec(memory_space=pltpu.HBM)] * count,
            out_specs=out_specs,
            scratch_shapes=scratch + [pltpu.SemaphoreType.DMA((count,))],
        ),
        out_shape=out_shape,
        compiler_params=pltpu.CompilerParams(vmem_limit_bytes=VMEM_BYTES),
        cost_estimate=cost,
    )(at, *early, *[pltpu.with_memory_space_constraint(p, pltpu.HBM) for p in pieces])


def gather_line(rows, axis):
    other = send(rows, k=1)
    first = send(rows, fan=axis)
    second = send(other, fan=axis)
    far = send(first, fan=axis)
    return [rows, other, first, send(first, k=1)], [second, far]


def both_cores(pieces):
    return pieces + [send(piece, k=1) for piece in pieces]


def reduce_line(sent, kept, axis, core):
    half, span = NZ // 2, 512

    def exponent(rows):
        return rows[:, -1:].astype(jnp.float32)

    def opened(rows):
        return rows[:, :-16].astype(jnp.float32) * jnp.exp2(-exponent(rows))

    def columns(value, core):
        return lax.dynamic_slice_in_dim(value, core * span, span, 1)

    received = send(sent, fan=axis)
    relay, plain = received[:half], received[half:]
    both = jnp.minimum(exponent(kept[0]), exponent(relay)) - 1.0
    is_exponent = jnp.arange(1040, dtype=jnp.int32)[None, :, None] >= 1024
    total = kept[0] + relay.astype(jnp.float32) * jnp.exp2(-exponent(relay))
    last = send(jnp.where(is_exponent, both, total * jnp.exp2(both)).astype(jnp.float16), fan=axis)
    plain = opened(plain)
    other_own, other_plain = send(
        jnp.stack([columns(kept[1], 1 - core), columns(plain, 1 - core)]), k=1
    )
    other_last = send(jnp.concatenate([columns(last, 1 - core), last[:, -16:]], axis=1), k=1)
    this_half = columns(kept[1], core) + other_plain + columns(opened(last), core)
    other_half = columns(plain, core) + other_own + opened(other_last)
    return jnp.concatenate(
        [jnp.where(core == 0, this_half, other_half), jnp.where(core == 0, other_half, this_half)], axis=0
    )


def reduce_z(value, beside):
    up, down = send(value[4, :1], z=1), send(value[4, 1:], z=-1)
    up = send(jnp.concatenate([value[3, :1] + up, value[3, 1:]], axis=0), z=1)
    down = send(jnp.concatenate([value[5, :1], value[5, 1:] + down], axis=0), z=-1)
    up, down, beside = lax.optimization_barrier((up, down, beside))
    up, down = send(value[2] + up, z=1), send(value[6] + down, z=-1)
    up, down = send(value[1] + up, z=1), send(value[7] + down, z=-1)
    return value[0] + up + down, beside


def body(acts, grads, lengths, assign):
    n_dp = lax.axis_size("dp")
    n_tile = lax.axis_size("tile")
    slot_count, block_len, feat_width = acts.shape
    dp, tile = lax.axis_index("dp"), lax.axis_index("tile")
    my_x, my_k = dp // NK, dp % NK
    my_z, my_y = tile // NY, tile % NY
    positions = jnp.arange(block_len, dtype=jnp.int32)
    live = (positions[:, None] < jnp.pad(lengths, (0, 16 - slot_count))[None, :])[:, :, None]
    rows_a, rows_g = token_rows(acts, live), token_rows(grads, live)
    early_a, late_a = gather_line(rows_a, "x")
    early_g, late_g = gather_line(rows_g, "y")

    scores = block_scores(rows_a, rows_g, block_len)[:slot_count]
    places = jnp.arange(n_dp * KEEP, dtype=jnp.int32)
    placed = jnp.sum(jnp.where(assign[:, None] == places[None, :], scores[:, None], 0.0), axis=0)
    got = lax.all_to_all(placed.reshape(n_dp, KEEP), "dp", split_axis=0, concat_axis=0, tiled=True)
    block_norms = jnp.sum(got, axis=0)

    at_a = jnp.stack([my_x, my_y, my_z, my_k])
    at_g = jnp.stack([my_y, my_x, my_z, my_k])
    sum_a, sum_g = product(True, at_a, early_a), product(False, at_g, early_g)
    late_a, late_g, sum_a, sum_g = lax.optimization_barrier((late_a, late_g, sum_a, sum_g))
    tokens = n_dp * slot_count * block_len
    sent_a, kept_a = product(True, at_a, both_cores(late_a), sum_a[::-1], tokens)
    sent_a = sent_a.astype(jnp.float16).reshape(NZ, 1040, 128)
    sent_a, kept_a, late_g, sum_g = lax.optimization_barrier((sent_a, kept_a, both_cores(late_g), sum_g))
    sent_g, kept_g = product(False, at_g, late_g, sum_g[::-1], tokens)
    sent_g = sent_g.astype(jnp.float16).reshape(NZ, 1040, 128)
    factor = 1.0 / (n_dp * n_tile * KEEP * block_len)
    line_a = reduce_line(sent_a, kept_a, "y", my_k) * factor
    line_g = reduce_line(sent_g, kept_g, "x", my_k) * factor
    total, block_norms = reduce_z(jnp.stack([line_a, line_g], axis=1), block_norms)
    act_factor = jnp.transpose(total[0])
    grad_factor = jnp.concatenate([total[1, at : at + 128] for at in range(0, 512, 128)], axis=1)
    return (act_factor, grad_factor, block_norms)


def solution(mesh):
    in_specs = (
        P(("dp", "tile"), None, None),
        P(("dp", "tile"), None, None),
        P(("dp", "tile")),
        P(("dp", "tile")),
    )
    out_specs = (P("tile", "dp"), P("tile", "dp"), P(("dp", "tile")))
    return jax.shard_map(body, mesh=mesh, in_specs=in_specs, out_specs=out_specs, check_vma=False)
```

```python
import functools

import jax
import jax.numpy as jnp
from jax import lax
from jax.experimental import pallas as pl
from jax.experimental.pallas import tpu as pltpu
from jax.sharding import PartitionSpec as P

KEEP = 12
NX, NK, NZ, NY = 4, 2, 8, 4
AXES = ("dp", "tile")
VMEM_BYTES = 26 * 1024 * 1024


def route(x=0, k=0, z=0, y=0, fan=None):
    pairs = []
    for sx in range(NX):
        for sk in range(NK):
            for sz in range(NZ):
                for sy in range(NY):
                    step = 1 - 2 * sk
                    tx = (sx + x + step * (fan == "x")) % NX
                    ty = (sy + y + step * (fan == "y")) % NY
                    tk, tz = (sk + k) % NK, (sz + z) % NZ
                    source = ((sx * NK + sk) * NZ + sz) * NY + sy
                    pairs.append((source, ((tx * NK + tk) * NZ + tz) * NY + ty))
    return pairs


def send(value, **shift):
    return lax.ppermute(value, AXES, route(**shift))


def token_rows(tokens, live):
    slots, count, width = tokens.shape
    by_position = jnp.pad(jnp.transpose(tokens, (1, 0, 2)), ((0, 0), (0, 16 - slots), (0, 0)))
    return jnp.where(live, by_position, 0).reshape(count * 16, width)


def block_scores(rows_a, rows_g, count):
    def gram(rows):
        return lax.dot_general(
            rows, rows, (((1,), (1,)), ((), ())), preferred_element_type=jnp.float32
        )

    slot = jnp.arange(rows_a.shape[0], dtype=jnp.int32) % 16
    same = slot[:, None] == slot[None, :]
    per_row = jnp.sum(jnp.where(same, gram(rows_a) * gram(rows_g), 0.0), axis=1)
    width = rows_a.shape[1]
    return jnp.sum(per_row.reshape(count, 16), axis=0) * (1.0 / (width * width * count))


def load(pieces, buf, sems):
    copies, start = [], 0
    for i, piece in enumerate(pieces):
        copies.append(pltpu.make_async_copy(piece, buf.at[pl.ds(start, piece.shape[0])], sems.at[i]))
        start += piece.shape[0]
    for copy in copies:
        copy.start()
    for copy in copies:
        copy.wait()


def largest(buf):
    def step(i, so_far):
        return jnp.maximum(so_far, jnp.abs(buf[pl.ds(pl.multiple_of(i * 16, 16), 16), :]))

    zeros = jnp.zeros((16, buf.shape[1]), buf.dtype)
    return jnp.max(lax.fori_loop(0, buf.shape[0] // 16, step, zeros).astype(jnp.float32))


def lanes(place):
    return pl.ds(pl.multiple_of(place * 128, 128), 128)


def load_and_turn(acts, at, pieces, buf, left, picked, sems):
    load(pieces, buf, sems)
    if acts:
        left[...] = jnp.transpose(buf[:, pl.ds(pl.multiple_of(at[0] * 1024, 1024), 1024)])
        for role in range(4):
            for i in range(4):
                unit = (role * 4 + i) * 128
                picked[:, unit : unit + 128] = buf[:, lanes(unit_tile(role, i, at))]
    else:
        for z in range(NZ):
            left[z * 128 : (z + 1) * 128, :] = jnp.transpose(buf[:, lanes(lax.rem(z + at[2], NZ) * 4 + at[0])])


def target_of(role, at):
    ahead = jnp.where(at[3] == 0, 1, 3)
    away = jnp.where(role == 0, 2, jnp.where(role == 3, 0, ahead))
    return lax.rem(at[1] + away, 4)


def half_of(role, at):
    return jnp.where(role == 1, 1 - at[3], at[3])


def unit_tile(role, i, at):
    z = lax.rem(half_of(role, at) * 4 + i + at[2], NZ)
    return z * 4 + target_of(role, at)


def products(acts, at, buf, left, picked, store):
    role = pl.program_id(0)
    if acts:
        columns = picked[:, pl.ds(pl.multiple_of(role * 512, 512), 512)]
        out = jnp.dot(left[...], columns, preferred_element_type=jnp.float32)
        for i in range(4):
            store(i, slice(0, 1024), out[:, i * 128 : (i + 1) * 128])
        return
    rows = left[pl.ds(pl.multiple_of(half_of(role, at) * 512, 512), 512), :]
    for core in range(2):
        start = pl.multiple_of((2 * target_of(role, at) + core) * 512, 512)
        out = jnp.dot(rows, buf[:, pl.ds(start, 512)], preferred_element_type=jnp.float32)
        for i in range(4):
            for part in range(4):
                tile = out[i * 128 : (i + 1) * 128, part * 128 : (part + 1) * 128]
                store(i, slice((core * 4 + part) * 128, (core * 4 + part + 1) * 128), tile)


def early_kernel(at, *refs, count, acts):
    pieces, (out, peak, buf, left, picked, sems) = refs[:count], refs[count:]

    @pl.when(pl.program_id(0) == 0)
    def _():
        load_and_turn(acts, at, pieces, buf, left, picked, sems)
        peak[...] = jnp.full(peak.shape, largest(buf), jnp.float32)

    def store(i, rows, value):
        out[0, i, rows] = value

    products(acts, at, buf, left, picked, store)


def late_kernel(at, early_peak, early, *refs, count, acts, tokens):
    pieces, (sent, kept, buf, left, picked, exponent, sems) = refs[:count], refs[count:]

    @pl.when(pl.program_id(0) == 0)
    def _():
        load_and_turn(acts, at, pieces, buf, left, picked, sems)
        peak = jnp.maximum(early_peak[0:1, :], largest(buf))
        bound = tokens * jnp.maximum(peak * peak, 1e-35)
        exponent[...] = jnp.broadcast_to(jnp.floor(jnp.log2(30000.0 / bound)), exponent.shape)

    def into(out, scale):
        def store(i, rows, value):
            out[0, i, rows] = (early[0, i, rows] + value) * scale

        products(acts, at, buf, left, picked, store)
        for i in range(4):
            out[0, i, 1024:1040] = exponent[...]

    @pl.when(pl.program_id(0) < 2)
    def _():
        into(sent, jnp.exp2(exponent[0:1, :]))

    @pl.when(pl.program_id(0) >= 2)
    def _():
        into(kept, 1.0)


def product(acts, at, pieces, early=(), tokens=None):
    count, rows, width = len(pieces), sum(p.shape[0] for p in pieces), pieces[0].shape[1]
    peak_spec = pl.BlockSpec((8, 128), lambda i, at: (0, 0))
    peak_shape = jax.ShapeDtypeStruct((8, 128), jnp.float32)
    spec = pl.BlockSpec((1, 4, 1024, 128), lambda i, at: (i, 0, 0, 0))
    scratch = [
        pltpu.VMEM((rows, width), jnp.bfloat16),
        pltpu.VMEM((1024, rows), jnp.bfloat16),
        pltpu.VMEM((rows, 2048) if acts else (16, 128), jnp.bfloat16),
    ]
    if early:
        kernel = functools.partial(late_kernel, tokens=tokens)
        before = [peak_spec, spec]
        out_specs = [
            pl.BlockSpec((1, 4, 1040, 128), lambda i, at: (jnp.minimum(i, 1), 0, 0, 0)),
            pl.BlockSpec((1, 4, 1040, 128), lambda i, at: (jnp.maximum(i - 2, 0), 0, 0, 0)),
        ]
        out_shape = [jax.ShapeDtypeStruct((2, 4, 1040, 128), jnp.float32)] * 2
        scratch.append(pltpu.VMEM((16, 128), jnp.float32))
        cost = pl.CostEstimate(
            flops=2 * rows * 1024 * 2048, bytes_accessed=2 * rows * width + 2 * 2048 * 4096, transcendentals=0
        )
    else:
        kernel, before = early_kernel, []
        out_specs = [spec, peak_spec]
        out_shape = [jax.ShapeDtypeStruct((4, 4, 1024, 128), jnp.float32), peak_shape]
        cost = pl.CostEstimate(flops=1, bytes_accessed=1, transcendentals=0)
    return pl.pallas_call(
        functools.partial(kernel, count=count, acts=acts),
        grid_spec=pltpu.PrefetchScalarGridSpec(
            num_scalar_prefetch=1,
            grid=(4,),
            in_specs=before + [pl.BlockSpec(memory_space=pltpu.HBM)] * count,
            out_specs=out_specs,
            scratch_shapes=scratch + [pltpu.SemaphoreType.DMA((count,))],
        ),
        out_shape=out_shape,
        compiler_params=pltpu.CompilerParams(vmem_limit_bytes=VMEM_BYTES),
        cost_estimate=cost,
    )(at, *early, *[pltpu.with_memory_space_constraint(p, pltpu.HBM) for p in pieces])


def gather_line(rows, axis):
    other = send(rows, k=1)
    first = send(rows, fan=axis)
    second = send(other, fan=axis)
    far = send(first, fan=axis)
    return [rows, other, first, send(first, k=1)], [second, far]


def both_cores(pieces):
    return pieces + [send(piece, k=1) for piece in pieces]


def exponent_of(rows):
    return rows[:, -1:].astype(jnp.float32)


def opened(rows):
    return rows[:, :-16].astype(jnp.float32) * jnp.exp2(-exponent_of(rows))


def relayed(kept, relay, exponent_rows):
    both = jnp.minimum(exponent_of(kept), exponent_of(relay)) - 1.0
    total = (kept + relay.astype(jnp.float32) * jnp.exp2(-exponent_of(relay))) * jnp.exp2(both)
    return jnp.where(exponent_rows, both, total).astype(jnp.float16)


def finish_line(own, plain, last, core, factor):
    def columns(value, core):
        return lax.dynamic_slice_in_dim(value, core * 512, 512, 1)

    plain = opened(plain)
    other_own, other_plain = send(jnp.stack([columns(own, 1 - core), columns(plain, 1 - core)]), k=1)
    other_last = send(jnp.concatenate([columns(last, 1 - core), last[:, -16:]], axis=1), k=1)
    this_half = (columns(own, core) + other_plain + columns(opened(last), core)) * factor
    other_half = (columns(plain, core) + other_own + opened(other_last)) * factor
    return jnp.where(core == 0, this_half, other_half), jnp.where(core == 0, other_half, this_half)


def reduce_z(low, high):
    up, down = send(high[0, :256], z=1), send(high[0, 256:], z=-1)
    up = send(jnp.concatenate([low[3, :256] + up, low[3, 256:]], axis=0), z=1)
    down = send(jnp.concatenate([high[1, :256], high[1, 256:] + down], axis=0), z=-1)
    up, down = send(low[2] + up, z=1), send(high[2] + down, z=-1)
    up, down = send(low[1] + up, z=1), send(high[3] + down, z=-1)
    return low[0] + up + down


def body(acts, grads, lengths, assign):
    n_dp = lax.axis_size("dp")
    n_tile = lax.axis_size("tile")
    slot_count, block_len, feat_width = acts.shape
    dp, tile = lax.axis_index("dp"), lax.axis_index("tile")
    my_x, my_k = dp // NK, dp % NK
    my_z, my_y = tile // NY, tile % NY
    positions = jnp.arange(block_len, dtype=jnp.int32)
    live = (positions[:, None] < jnp.pad(lengths, (0, 16 - slot_count))[None, :])[:, :, None]
    rows_a, rows_g = token_rows(acts, live), token_rows(grads, live)
    early_a, late_a = gather_line(rows_a, "x")
    early_g, late_g = gather_line(rows_g, "y")

    scores = block_scores(rows_a, rows_g, block_len)[:slot_count]
    places = jnp.arange(n_dp * KEEP, dtype=jnp.int32)
    placed = jnp.sum(jnp.where(assign[:, None] == places[None, :], scores[:, None], 0.0), axis=0)
    at_a = jnp.stack([my_x, my_y, my_z, my_k])
    at_g = jnp.stack([my_y, my_x, my_z, my_k])
    sum_a, sum_g = product(True, at_a, early_a), product(False, at_g, early_g)
    late_a, late_g, sum_a, sum_g, placed = lax.optimization_barrier((late_a, late_g, sum_a, sum_g, placed))
    late_a, late_g = both_cores(late_a), both_cores(late_g)
    placed = lax.all_to_all(placed.reshape(n_dp, KEEP), "dp", split_axis=0, concat_axis=0, tiled=True)
    block_norms = jnp.sum(placed, axis=0)
    late_a, block_norms = lax.optimization_barrier((late_a, block_norms))
    tokens = n_dp * slot_count * block_len
    sent_a, kept_a = product(True, at_a, late_a, sum_a[::-1], tokens)
    sent_a = sent_a.astype(jnp.float16).reshape(NZ, 1040, 128)
    sent_a, kept_a, late_g, sum_g = lax.optimization_barrier((sent_a, kept_a, late_g, sum_g))
    sent_g, kept_g = product(False, at_g, late_g, sum_g[::-1], tokens)
    sent_g = sent_g.astype(jnp.float16).reshape(NZ, 1040, 128)
    got_a, got_g = send(sent_a, fan="y"), send(sent_g, fan="x")
    row = jnp.arange(1040, dtype=jnp.int32)[None, :, None]
    last_a = send(relayed(kept_a[0], got_a[:4], row >= 1024), fan="y")
    last_g = send(relayed(kept_g[0], got_g[:4], row // 16 == 64), fan="x")
    factor = 1.0 / (n_dp * n_tile * KEEP * block_len)
    act_factor = jnp.transpose(reduce_z(*finish_line(kept_a[1], got_a[4:], last_a, my_k, factor)))
    total_g = reduce_z(*finish_line(kept_g[1], got_g[4:], last_g, my_k, factor))
    grad_factor = jnp.concatenate([total_g[at : at + 128] for at in range(0, 512, 128)], axis=1)
    return (act_factor, grad_factor, block_norms)


def solution(mesh):
    in_specs = (
        P(("dp", "tile"), None, None),
        P(("dp", "tile"), None, None),
        P(("dp", "tile")),
        P(("dp", "tile")),
    )
    out_specs = (P("tile", "dp"), P("tile", "dp"), P(("dp", "tile")))
    return jax.shard_map(body, mesh=mesh, in_specs=in_specs, out_specs=out_specs, check_vma=False)
```

```python
import functools

import jax
import jax.numpy as jnp
from jax import lax
from jax.experimental import pallas as pl
from jax.experimental.pallas import tpu as pltpu
from jax.sharding import PartitionSpec as P

KEEP = 12
NX, NK, NZ, NY = 4, 2, 8, 4
AXES = ("dp", "tile")
VMEM_BYTES = 18 * 1024 * 1024


def route(x=0, k=0, z=0, y=0, fan=None):
    pairs = []
    for sx in range(NX):
        for sk in range(NK):
            for sz in range(NZ):
                for sy in range(NY):
                    step = 1 - 2 * sk
                    tx = (sx + x + step * (fan == "x")) % NX
                    ty = (sy + y + step * (fan == "y")) % NY
                    tk, tz = (sk + k) % NK, (sz + z) % NZ
                    source = ((sx * NK + sk) * NZ + sz) * NY + sy
                    pairs.append((source, ((tx * NK + tk) * NZ + tz) * NY + ty))
    return pairs


def send(value, **shift):
    return lax.ppermute(value, AXES, route(**shift))


def token_rows(tokens, live):
    slots, count, width = tokens.shape
    by_position = jnp.pad(jnp.transpose(tokens, (1, 0, 2)), ((0, 0), (0, 16 - slots), (0, 0)))
    return jnp.where(live, by_position, 0).reshape(count * 16, width)


def block_scores(rows_a, rows_g, count):
    def gram(rows):
        return lax.dot_general(
            rows, rows, (((1,), (1,)), ((), ())), preferred_element_type=jnp.float32
        )

    slot = jnp.arange(rows_a.shape[0], dtype=jnp.int32) % 16
    same = slot[:, None] == slot[None, :]
    per_row = jnp.sum(jnp.where(same, gram(rows_a) * gram(rows_g), 0.0), axis=1)
    width = rows_a.shape[1]
    return jnp.sum(per_row.reshape(count, 16), axis=0) * (1.0 / (width * width * count))


def load(pieces, buf, sems):
    copies, start = [], 0
    for i, piece in enumerate(pieces):
        copies.append(pltpu.make_async_copy(piece, buf.at[pl.ds(start, piece.shape[0])], sems.at[i]))
        start += piece.shape[0]
    for copy in copies:
        copy.start()
    for copy in copies:
        copy.wait()


def largest(buf):
    def step(i, so_far):
        return jnp.maximum(so_far, jnp.abs(buf[pl.ds(pl.multiple_of(i * 16, 16), 16), :]))

    zeros = jnp.zeros((16, buf.shape[1]), buf.dtype)
    return jnp.max(lax.fori_loop(0, buf.shape[0] // 16, step, zeros).astype(jnp.float32))


def lanes(place):
    return pl.ds(pl.multiple_of(place * 128, 128), 128)


def load_and_turn(acts, at, pieces, buf, left, sems):
    load(pieces, buf, sems)
    if acts:
        left[...] = jnp.transpose(buf[:, pl.ds(pl.multiple_of(at[0] * 1024, 1024), 1024)])
    else:
        for z in range(NZ):
            left[z * 128 : (z + 1) * 128, :] = jnp.transpose(buf[:, lanes(lax.rem(z + at[2], NZ) * 4 + at[0])])


def target_of(role, at):
    ahead = jnp.where(at[3] == 0, 1, 3)
    away = jnp.where(role == 0, 2, jnp.where(role == 3, 0, ahead))
    return lax.rem(at[1] + away, 4)


def half_of(role, at):
    return jnp.where(role == 1, 1 - at[3], at[3])


def unit_tile(role, i, at):
    z = lax.rem(half_of(role, at) * 4 + i + at[2], NZ)
    return z * 4 + target_of(role, at)


def products(acts, at, buf, left, store):
    role, first = pl.program_id(0) // 2, lax.rem(pl.program_id(0), 2) * 2
    if acts:
        columns = jnp.concatenate([buf[:, lanes(unit_tile(role, first + i, at))] for i in range(2)], axis=1)
        out = jnp.dot(left[...], columns, preferred_element_type=jnp.float32)
        for i in range(2):
            store(i, slice(0, 1024), out[:, i * 128 : (i + 1) * 128])
        return
    rows = left[pl.ds(pl.multiple_of(half_of(role, at) * 512 + first * 128, 256), 256), :]
    for core in range(2):
        start = pl.multiple_of((2 * target_of(role, at) + core) * 512, 512)
        out = jnp.dot(rows, buf[:, pl.ds(start, 512)], preferred_element_type=jnp.float32)
        for i in range(2):
            for part in range(4):
                tile = out[i * 128 : (i + 1) * 128, part * 128 : (part + 1) * 128]
                store(i, slice((core * 4 + part) * 128, (core * 4 + part + 1) * 128), tile)


def early_kernel(at, *refs, count, acts):
    pieces, (out, peak, buf, left, sems) = refs[:count], refs[count:]

    @pl.when(pl.program_id(0) == 0)
    def _():
        load_and_turn(acts, at, pieces, buf, left, sems)
        peak[...] = jnp.full(peak.shape, largest(buf), jnp.float32)

    def store(i, rows, value):
        out[0, i, rows] = value

    products(acts, at, buf, left, store)


def late_kernel(at, early_peak, early, *refs, count, acts, tokens):
    pieces, (sent, kept, buf, left, exponent, sems) = refs[:count], refs[count:]

    @pl.when(pl.program_id(0) == 0)
    def _():
        load_and_turn(acts, at, pieces, buf, left, sems)
        peak = jnp.maximum(early_peak[0:1, :], largest(buf))
        bound = tokens * jnp.maximum(peak * peak, 1e-35)
        exponent[...] = jnp.broadcast_to(jnp.floor(jnp.log2(30000.0 / bound)), exponent.shape)

    def into(out, scale):
        def store(i, rows, value):
            out[0, i, rows] = (early[0, i, rows] + value) * scale

        products(acts, at, buf, left, store)
        for i in range(2):
            out[0, i, 1024:1040] = exponent[...]

    @pl.when(pl.program_id(0) < 4)
    def _():
        into(sent, jnp.exp2(exponent[0:1, :]))

    @pl.when(pl.program_id(0) >= 4)
    def _():
        into(kept, 1.0)


def halves(step):
    return step // 2, lax.rem(step, 2), 0, 0


def product(acts, at, pieces, early=(), tokens=None):
    count, rows, width = len(pieces), sum(p.shape[0] for p in pieces), pieces[0].shape[1]
    peak_spec = pl.BlockSpec((8, 128), lambda i, at: (0, 0))
    peak_shape = jax.ShapeDtypeStruct((8, 128), jnp.float32)
    spec = pl.BlockSpec((1, 2, 1024, 128), lambda i, at: halves(i))
    scratch = [
        pltpu.VMEM((rows, width), jnp.bfloat16),
        pltpu.VMEM((1024, rows), jnp.bfloat16),
    ]
    if early:
        kernel = functools.partial(late_kernel, tokens=tokens)
        before = [peak_spec, spec]
        out_specs = [
            pl.BlockSpec((1, 2, 1040, 128), lambda i, at: halves(jnp.minimum(i, 3))),
            pl.BlockSpec((1, 2, 1040, 128), lambda i, at: halves(jnp.maximum(i - 4, 0))),
        ]
        out_shape = [jax.ShapeDtypeStruct((2, 4, 1040, 128), jnp.float32)] * 2
        scratch.append(pltpu.VMEM((16, 128), jnp.float32))
        cost = pl.CostEstimate(
            flops=2 * rows * 1024 * 2048, bytes_accessed=2 * rows * width + 2 * 2048 * 4096, transcendentals=0
        )
    else:
        kernel, before = early_kernel, []
        out_specs = [spec, peak_spec]
        out_shape = [jax.ShapeDtypeStruct((4, 4, 1024, 128), jnp.float32), peak_shape]
        cost = pl.CostEstimate(flops=1, bytes_accessed=1, transcendentals=0)
    return pl.pallas_call(
        functools.partial(kernel, count=count, acts=acts),
        grid_spec=pltpu.PrefetchScalarGridSpec(
            num_scalar_prefetch=1,
            grid=(8,),
            in_specs=before + [pl.BlockSpec(memory_space=pltpu.HBM)] * count,
            out_specs=out_specs,
            scratch_shapes=scratch + [pltpu.SemaphoreType.DMA((count,))],
        ),
        out_shape=out_shape,
        compiler_params=pltpu.CompilerParams(vmem_limit_bytes=VMEM_BYTES),
        cost_estimate=cost,
    )(at, *early, *[pltpu.with_memory_space_constraint(p, pltpu.HBM) for p in pieces])


def gather_line(rows, axis):
    other = send(rows, k=1)
    first = send(rows, fan=axis)
    second = send(other, fan=axis)
    far = send(first, fan=axis)
    return [rows, other, first, send(first, k=1)], [second, far]


def both_cores(pieces):
    return pieces + [send(piece, k=1) for piece in pieces]


def exponent_of(rows):
    return rows[:, -1:].astype(jnp.float32)


def opened(rows):
    return rows[:, :-16].astype(jnp.float32) * jnp.exp2(-exponent_of(rows))


def relayed(kept, relay, exponent_rows):
    both = jnp.minimum(exponent_of(kept), exponent_of(relay)) - 1.0
    total = (kept + relay.astype(jnp.float32) * jnp.exp2(-exponent_of(relay))) * jnp.exp2(both)
    return jnp.where(exponent_rows, both, total).astype(jnp.float16)


def finish_line(own, plain, last, core, factor):
    def columns(value, core):
        return lax.dynamic_slice_in_dim(value, core * 512, 512, 1)

    plain = opened(plain)
    other_own, other_plain = send(jnp.stack([columns(own, 1 - core), columns(plain, 1 - core)]), k=1)
    other_last = send(jnp.concatenate([columns(last, 1 - core), last[:, -16:]], axis=1), k=1)
    this_half = (columns(own, core) + other_plain + columns(opened(last), core)) * factor
    other_half = (columns(plain, core) + other_own + opened(other_last)) * factor
    return jnp.where(core == 0, this_half, other_half), jnp.where(core == 0, other_half, this_half)


def reduce_z(low, high):
    up, down = send(high[0, :256], z=1), send(high[0, 256:], z=-1)
    up = send(jnp.concatenate([low[3, :256] + up, low[3, 256:]], axis=0), z=1)
    down = send(jnp.concatenate([high[1, :256], high[1, 256:] + down], axis=0), z=-1)
    up, down = send(low[2] + up, z=1), send(high[2] + down, z=-1)
    up, down = send(low[1] + up, z=1), send(high[3] + down, z=-1)
    return low[0] + up + down


def body(acts, grads, lengths, assign):
    n_dp = lax.axis_size("dp")
    n_tile = lax.axis_size("tile")
    slot_count, block_len, feat_width = acts.shape
    dp, tile = lax.axis_index("dp"), lax.axis_index("tile")
    my_x, my_k = dp // NK, dp % NK
    my_z, my_y = tile // NY, tile % NY
    positions = jnp.arange(block_len, dtype=jnp.int32)
    live = (positions[:, None] < jnp.pad(lengths, (0, 16 - slot_count))[None, :])[:, :, None]
    rows_a, rows_g = token_rows(acts, live), token_rows(grads, live)
    early_a, late_a = gather_line(rows_a, "x")
    early_g, late_g = gather_line(rows_g, "y")

    scores = block_scores(rows_a, rows_g, block_len)[:slot_count]
    places = jnp.arange(n_dp * KEEP, dtype=jnp.int32)
    placed = jnp.sum(jnp.where(assign[:, None] == places[None, :], scores[:, None], 0.0), axis=0)
    at_a = jnp.stack([my_x, my_y, my_z, my_k])
    at_g = jnp.stack([my_y, my_x, my_z, my_k])
    sum_a, sum_g = product(True, at_a, early_a), product(False, at_g, early_g)
    sum_a, sum_g, placed = lax.optimization_barrier((sum_a, sum_g, placed))
    placed = lax.all_to_all(placed.reshape(n_dp, KEEP), "dp", split_axis=0, concat_axis=0, tiled=True)
    block_norms = jnp.sum(placed, axis=0)
    late_a, late_g, sum_a, sum_g, block_norms = lax.optimization_barrier(
        (late_a, late_g, sum_a, sum_g, block_norms)
    )
    late_a, late_g = both_cores(late_a), both_cores(late_g)
    tokens = n_dp * slot_count * block_len
    sent_a, kept_a = product(True, at_a, late_a, sum_a[::-1], tokens)
    relay_a = sent_a[0].astype(jnp.float16)
    relay_a, sent_a, kept_a, late_g, sum_g = lax.optimization_barrier((relay_a, sent_a, kept_a, late_g, sum_g))
    sent_g, kept_g = product(False, at_g, late_g, sum_g[::-1], tokens)
    row = jnp.arange(1040, dtype=jnp.int32)[None, :, None]

    def send_on(relay, sent, kept, exponent_rows, axis):
        last = relayed(kept[0], send(relay, fan=axis), exponent_rows)
        last, sent = lax.optimization_barrier((last, sent))
        return send(last, fan=axis), send(sent[1].astype(jnp.float16), fan=axis)

    last_a, plain_a = send_on(relay_a, sent_a, kept_a, row >= 1024, "y")
    last_g, plain_g = send_on(sent_g[0].astype(jnp.float16), sent_g, kept_g, row // 16 == 64, "x")
    factor = 1.0 / (n_dp * n_tile * KEEP * block_len)
    act_factor = jnp.transpose(reduce_z(*finish_line(kept_a[1], plain_a, last_a, my_k, factor)))
    total_g = reduce_z(*finish_line(kept_g[1], plain_g, last_g, my_k, factor))
    grad_factor = jnp.concatenate([total_g[at : at + 128] for at in range(0, 512, 128)], axis=1)
    return (act_factor, grad_factor, block_norms)


def solution(mesh):
    in_specs = (
        P(("dp", "tile"), None, None),
        P(("dp", "tile"), None, None),
        P(("dp", "tile")),
        P(("dp", "tile")),
    )
    out_specs = (P("tile", "dp"), P("tile", "dp"), P(("dp", "tile")))
    return jax.shard_map(body, mesh=mesh, in_specs=in_specs, out_specs=out_specs, check_vma=False)
```

```python
import functools

import jax
import jax.numpy as jnp
from jax import lax
from jax.experimental import pallas as pl
from jax.experimental.pallas import tpu as pltpu
from jax.sharding import PartitionSpec as P

KEEP = 12
NX, NK, NZ, NY = 4, 2, 8, 4
AXES = ("dp", "tile")
VMEM_BYTES = 24 * 1024 * 1024


def route(x=0, k=0, z=0, y=0, fan=None):
    pairs = []
    for sx in range(NX):
        for sk in range(NK):
            for sz in range(NZ):
                for sy in range(NY):
                    step = 1 - 2 * sk
                    tx = (sx + x + step * (fan == "x")) % NX
                    ty = (sy + y + step * (fan == "y")) % NY
                    tk, tz = (sk + k) % NK, (sz + z) % NZ
                    source = ((sx * NK + sk) * NZ + sz) * NY + sy
                    pairs.append((source, ((tx * NK + tk) * NZ + tz) * NY + ty))
    return pairs


def send(value, **shift):
    return lax.ppermute(value, AXES, route(**shift))


def token_rows(tokens, live):
    slots, count, width = tokens.shape
    by_position = jnp.pad(jnp.transpose(tokens, (1, 0, 2)), ((0, 0), (0, 16 - slots), (0, 0)))
    return jnp.where(live, by_position, 0).reshape(count * 16, width)


def block_scores(rows_a, rows_g, count):
    def gram(rows):
        return lax.dot_general(
            rows, rows, (((1,), (1,)), ((), ())), preferred_element_type=jnp.float32
        )

    slot = jnp.arange(rows_a.shape[0], dtype=jnp.int32) % 16
    same = slot[:, None] == slot[None, :]
    per_row = jnp.sum(jnp.where(same, gram(rows_a) * gram(rows_g), 0.0), axis=1)
    width = rows_a.shape[1]
    return jnp.sum(per_row.reshape(count, 16), axis=0) * (1.0 / (width * width * count))


def load(pieces, buf, sems):
    copies, start = [], 0
    for i, piece in enumerate(pieces):
        copies.append(pltpu.make_async_copy(piece, buf.at[pl.ds(start, piece.shape[0])], sems.at[i]))
        copies[-1].start()
        start += piece.shape[0]
    return copies


def largest(buf):
    def step(i, so_far):
        return jnp.maximum(so_far, jnp.abs(buf[pl.ds(pl.multiple_of(i * 16, 16), 16), :]))

    zeros = jnp.zeros((16, buf.shape[1]), buf.dtype)
    return jnp.max(lax.fori_loop(0, buf.shape[0] // 16, step, zeros).astype(jnp.float32))


def lanes(place):
    return pl.ds(pl.multiple_of(place * 128, 128), 128)


def load_and_turn(acts, at, pieces, buf, left, sems, meanwhile=lambda: None):
    copies = load(pieces, buf, sems)
    meanwhile()
    for first in range(0, len(pieces), 2):
        copies[first].wait()
        copies[first + 1].wait()
        here = slice(first * pieces[0].shape[0], (first + 2) * pieces[0].shape[0])
        if acts:
            left[:, here] = jnp.transpose(buf[here, pl.ds(pl.multiple_of(at[0] * 1024, 1024), 1024)])
        else:
            for z in range(NZ):
                tile = lanes(lax.rem(z + at[2], NZ) * 4 + at[0])
                left[z * 128 : (z + 1) * 128, here] = jnp.transpose(buf[here, tile])


def target_of(role, at):
    ahead = jnp.where(at[3] == 0, 1, 3)
    away = jnp.where(role == 0, 2, jnp.where(role == 3, 0, ahead))
    return lax.rem(at[1] + away, 4)


def half_of(role, at):
    return jnp.where(role == 1, 1 - at[3], at[3])


def unit_tile(role, i, at):
    z = lax.rem(half_of(role, at) * 4 + i + at[2], NZ)
    return z * 4 + target_of(role, at)


def products(acts, at, buf, left, store):
    role, first = pl.program_id(0) // 2, lax.rem(pl.program_id(0), 2) * 2
    if acts:
        columns = jnp.concatenate([buf[:, lanes(unit_tile(role, first + i, at))] for i in range(2)], axis=1)
        out = jnp.dot(left[...], columns, preferred_element_type=jnp.float32)
        for i in range(2):
            store(i, slice(0, 1024), out[:, i * 128 : (i + 1) * 128])
        return
    rows = left[pl.ds(pl.multiple_of(half_of(role, at) * 512 + first * 128, 256), 256), :]
    for core in range(2):
        start = pl.multiple_of((2 * target_of(role, at) + core) * 512, 512)
        out = jnp.dot(rows, buf[:, pl.ds(start, 512)], preferred_element_type=jnp.float32)
        for i in range(2):
            for part in range(4):
                tile = out[i * 128 : (i + 1) * 128, part * 128 : (part + 1) * 128]
                store(i, slice((core * 4 + part) * 128, (core * 4 + part + 1) * 128), tile)


def early_kernel(at, *refs, count, acts):
    pieces, (out, peak, buf, left, sems) = refs[:count], refs[count:]

    @pl.when(pl.program_id(0) == 0)
    def _():
        load_and_turn(acts, at, pieces, buf, left, sems)
        peak[...] = jnp.full(peak.shape, largest(buf), jnp.float32)

    def store(i, rows, value):
        out[0, i, rows] = value

    products(acts, at, buf, left, store)


def late_kernel(at, early_peak, early, *refs, count, acts, tokens):
    pieces, (sent, kept, buf, left, exponent, sums, sums_sems, sems) = refs[:count], refs[count:]
    step = pl.program_id(0)

    def fetch(i):
        part = early.at[i // 2, pl.ds(lax.rem(i, 2) * 2, 2)]
        return pltpu.make_async_copy(part, sums.at[i], sums_sems.at[i])

    @pl.when(step == 0)
    def _():
        def fetch_all():
            for i in range(8):
                fetch(jnp.int32(i)).start()

        load_and_turn(acts, at, pieces, buf, left, sems, fetch_all)
        peak = jnp.maximum(early_peak[0:1, :], largest(buf))
        bound = tokens * jnp.maximum(peak * peak, 1e-35)
        exponent[...] = jnp.broadcast_to(jnp.floor(jnp.log2(30000.0 / bound)), exponent.shape)

    fetch(step).wait()

    def into(out, scale):
        def store(i, rows, value):
            out[0, i, rows] = (sums[step, i, rows] + value) * scale

        products(acts, at, buf, left, store)
        for i in range(2):
            out[0, i, 1024:1040] = exponent[...]

    @pl.when(pl.program_id(0) < 4)
    def _():
        into(sent, jnp.exp2(exponent[0:1, :]))

    @pl.when(pl.program_id(0) >= 4)
    def _():
        into(kept, 1.0)


def halves(step):
    return step // 2, lax.rem(step, 2), 0, 0


def product(acts, at, pieces, early=(), tokens=None):
    count, rows, width = len(pieces), sum(p.shape[0] for p in pieces), pieces[0].shape[1]
    peak_spec = pl.BlockSpec((8, 128), lambda i, at: (0, 0))
    peak_shape = jax.ShapeDtypeStruct((8, 128), jnp.float32)
    spec = pl.BlockSpec((1, 2, 1024, 128), lambda i, at: halves(i))
    scratch = [
        pltpu.VMEM((rows, width), jnp.bfloat16),
        pltpu.VMEM((1024, rows), jnp.bfloat16),
    ]
    if early:
        kernel = functools.partial(late_kernel, tokens=tokens)
        before = [peak_spec, pl.BlockSpec(memory_space=pltpu.HBM)]
        out_specs = [
            pl.BlockSpec((1, 2, 1040, 128), lambda i, at: halves(jnp.minimum(i, 3))),
            pl.BlockSpec((1, 2, 1040, 128), lambda i, at: halves(jnp.maximum(i - 4, 0))),
        ]
        out_shape = [jax.ShapeDtypeStruct((2, 4, 1040, 128), jnp.float32)] * 2
        scratch += [
            pltpu.VMEM((16, 128), jnp.float32),
            pltpu.VMEM((8, 2, 1024, 128), jnp.float32),
            pltpu.SemaphoreType.DMA((8,)),
        ]
        cost = pl.CostEstimate(
            flops=2 * rows * 1024 * 2048, bytes_accessed=2 * rows * width + 2 * 2048 * 4096, transcendentals=0
        )
    else:
        kernel, before = early_kernel, []
        out_specs = [spec, peak_spec]
        out_shape = [pltpu.HBM((4, 4, 1024, 128), jnp.float32), peak_shape]
        cost = pl.CostEstimate(flops=1, bytes_accessed=1, transcendentals=0)
    return pl.pallas_call(
        functools.partial(kernel, count=count, acts=acts),
        grid_spec=pltpu.PrefetchScalarGridSpec(
            num_scalar_prefetch=1,
            grid=(8,),
            in_specs=before + [pl.BlockSpec(memory_space=pltpu.HBM)] * count,
            out_specs=out_specs,
            scratch_shapes=scratch + [pltpu.SemaphoreType.DMA((count,))],
        ),
        out_shape=out_shape,
        compiler_params=pltpu.CompilerParams(vmem_limit_bytes=VMEM_BYTES),
        cost_estimate=cost,
    )(at, *early[:1], *[pltpu.with_memory_space_constraint(p, pltpu.HBM) for p in (*early[1:], *pieces)])


def gather_line(rows, axis):
    other = send(rows, k=1)
    first = send(rows, fan=axis)
    second = send(other, fan=axis)
    far = send(first, fan=axis)
    return [rows, other, first, send(first, k=1)], [second, far]


def both_cores(pieces):
    return pieces + [send(piece, k=1) for piece in pieces]


def exponent_of(rows):
    return rows[:, -1:].astype(jnp.float32)


def opened(rows):
    return rows[:, :-16].astype(jnp.float32) * jnp.exp2(-exponent_of(rows))


def relayed(kept, relay, exponent_rows):
    both = jnp.minimum(exponent_of(kept), exponent_of(relay)) - 1.0
    total = (kept + relay.astype(jnp.float32) * jnp.exp2(-exponent_of(relay))) * jnp.exp2(both)
    return jnp.where(exponent_rows, both, total).astype(jnp.float16)


def finish_line(own, plain, last, core, factor):
    def columns(value, core):
        return lax.dynamic_slice_in_dim(value, core * 512, 512, 1)

    plain = opened(plain)
    other_own, other_plain = send(jnp.stack([columns(own, 1 - core), columns(plain, 1 - core)]), k=1)
    other_last = send(jnp.concatenate([columns(last, 1 - core), last[:, -16:]], axis=1), k=1)
    this_half = (columns(own, core) + other_plain + columns(opened(last), core)) * factor
    other_half = (columns(plain, core) + other_own + opened(other_last)) * factor
    return jnp.where(core == 0, this_half, other_half), jnp.where(core == 0, other_half, this_half)


def reduce_z(low, high):
    up, down = send(high[0, :256], z=1), send(high[0, 256:], z=-1)
    up = send(jnp.concatenate([low[3, :256] + up, low[3, 256:]], axis=0), z=1)
    down = send(jnp.concatenate([high[1, :256], high[1, 256:] + down], axis=0), z=-1)
    up, down = send(low[2] + up, z=1), send(high[2] + down, z=-1)
    up, down = send(low[1] + up, z=1), send(high[3] + down, z=-1)
    return low[0] + up + down


def body(acts, grads, lengths, assign):
    n_dp = lax.axis_size("dp")
    n_tile = lax.axis_size("tile")
    slot_count, block_len, feat_width = acts.shape
    dp, tile = lax.axis_index("dp"), lax.axis_index("tile")
    my_x, my_k = dp // NK, dp % NK
    my_z, my_y = tile // NY, tile % NY
    positions = jnp.arange(block_len, dtype=jnp.int32)
    live = (positions[:, None] < jnp.pad(lengths, (0, 16 - slot_count))[None, :])[:, :, None]
    rows_a, rows_g = token_rows(acts, live), token_rows(grads, live)
    early_a, late_a = gather_line(rows_a, "x")
    early_g, late_g = gather_line(rows_g, "y")

    scores = block_scores(rows_a, rows_g, block_len)[:slot_count]
    places = jnp.arange(n_dp * KEEP, dtype=jnp.int32)
    placed = jnp.sum(jnp.where(assign[:, None] == places[None, :], scores[:, None], 0.0), axis=0)
    at_a = jnp.stack([my_x, my_y, my_z, my_k])
    at_g = jnp.stack([my_y, my_x, my_z, my_k])
    sum_a, sum_g = product(True, at_a, early_a), product(False, at_g, early_g)
    sum_a, sum_g, placed = lax.optimization_barrier((sum_a, sum_g, placed))
    placed = lax.all_to_all(placed.reshape(n_dp, KEEP), "dp", split_axis=0, concat_axis=0, tiled=True)
    block_norms = jnp.sum(placed, axis=0)
    late_a, late_g, sum_a, sum_g, block_norms = lax.optimization_barrier(
        (late_a, late_g, sum_a, sum_g, block_norms)
    )
    late_a, late_g = both_cores(late_a), both_cores(late_g)
    tokens = n_dp * slot_count * block_len
    sent_a, kept_a = product(True, at_a, late_a, sum_a[::-1], tokens)
    relay_a = sent_a[0].astype(jnp.float16)
    relay_a, sent_a, kept_a, late_g, sum_g = lax.optimization_barrier((relay_a, sent_a, kept_a, late_g, sum_g))
    sent_g, kept_g = product(False, at_g, late_g, sum_g[::-1], tokens)
    row = jnp.arange(1040, dtype=jnp.int32)[None, :, None]

    def send_on(relay, sent, kept, exponent_rows, axis):
        last = relayed(kept[0], send(relay, fan=axis), exponent_rows)
        last, sent = lax.optimization_barrier((last, sent))
        return send(last, fan=axis), send(sent[1].astype(jnp.float16), fan=axis)

    last_a, plain_a = send_on(relay_a, sent_a, kept_a, row >= 1024, "y")
    last_g, plain_g = send_on(sent_g[0].astype(jnp.float16), sent_g, kept_g, row // 16 == 64, "x")
    factor = 1.0 / (n_dp * n_tile * KEEP * block_len)
    act_factor = jnp.transpose(reduce_z(*finish_line(kept_a[1], plain_a, last_a, my_k, factor)))
    total_g = reduce_z(*finish_line(kept_g[1], plain_g, last_g, my_k, factor))
    grad_factor = jnp.concatenate([total_g[at : at + 128] for at in range(0, 512, 128)], axis=1)
    return (act_factor, grad_factor, block_norms)


def solution(mesh):
    in_specs = (
        P(("dp", "tile"), None, None),
        P(("dp", "tile"), None, None),
        P(("dp", "tile")),
        P(("dp", "tile")),
    )
    out_specs = (P("tile", "dp"), P("tile", "dp"), P(("dp", "tile")))
    return jax.shard_map(body, mesh=mesh, in_specs=in_specs, out_specs=out_specs, check_vma=False)
```

```python
import functools

import jax
import jax.numpy as jnp
from jax import lax
from jax.experimental import pallas as pl
from jax.experimental.pallas import tpu as pltpu
from jax.sharding import PartitionSpec as P

KEEP = 12
NX, NK, NZ, NY = 4, 2, 8, 4
AXES = ("dp", "tile")
VMEM_BYTES = 24 * 1024 * 1024


def route(x=0, k=0, z=0, y=0, fan=None):
    pairs = []
    for sx in range(NX):
        for sk in range(NK):
            for sz in range(NZ):
                for sy in range(NY):
                    step = 1 - 2 * sk
                    tx = (sx + x + step * (fan == "x")) % NX
                    ty = (sy + y + step * (fan == "y")) % NY
                    tk, tz = (sk + k) % NK, (sz + z) % NZ
                    source = ((sx * NK + sk) * NZ + sz) * NY + sy
                    pairs.append((source, ((tx * NK + tk) * NZ + tz) * NY + ty))
    return pairs


def send(value, **shift):
    return lax.ppermute(value, AXES, route(**shift))


def token_rows(tokens, live):
    slots, count, width = tokens.shape
    by_position = jnp.pad(jnp.transpose(tokens, (1, 0, 2)), ((0, 0), (0, 16 - slots), (0, 0)))
    return jnp.where(live, by_position, 0).reshape(count * 16, width)


def score_kernel(rows_a, rows_g, out, gram_a, gram_g):
    gram_a[...] = jnp.zeros_like(gram_a)
    gram_g[...] = jnp.zeros_like(gram_g)

    def add(i, _):
        part = pl.ds(pl.multiple_of(i * 512, 512), 512)
        for rows, gram in ((rows_a, gram_a), (rows_g, gram_g)):
            values = rows[:, part]
            gram[...] += lax.dot_general(
                values, values, (((1,), (1,)), ((), ())), preferred_element_type=jnp.float32
            )
        return 0

    lax.fori_loop(0, rows_a.shape[1] // 512, add, 0)
    row, column = (lax.broadcasted_iota(jnp.int32, gram_a.shape, dim) for dim in (0, 1))
    both = jnp.where((row & 15) == (column & 15), gram_a[...] * gram_g[...], 0.0)
    out[...] = jnp.broadcast_to(jnp.sum(both, axis=0, keepdims=True), out.shape)


def block_scores(rows_a, rows_g, count):
    rows, width = rows_a.shape
    sums = pl.pallas_call(
        score_kernel,
        out_shape=jax.ShapeDtypeStruct((8, rows), jnp.float32),
        in_specs=[pl.BlockSpec(memory_space=pltpu.VMEM)] * 2,
        scratch_shapes=[pltpu.VMEM((rows, rows), jnp.float32)] * 2,
        compiler_params=pltpu.CompilerParams(vmem_limit_bytes=VMEM_BYTES),
        cost_estimate=pl.CostEstimate(flops=1, bytes_accessed=1, transcendentals=0),
    )(rows_a, rows_g)
    return jnp.sum(sums[0].reshape(count, 16), axis=0) * (1.0 / (width * width * count))


def load(pieces, buf, sems):
    copies, start = [], 0
    for i, piece in enumerate(pieces):
        copies.append(pltpu.make_async_copy(piece, buf.at[pl.ds(start, piece.shape[0])], sems.at[i]))
        copies[-1].start()
        start += piece.shape[0]
    return copies


def largest(buf):
    def step(i, so_far):
        return jnp.maximum(so_far, jnp.abs(buf[pl.ds(pl.multiple_of(i * 16, 16), 16), :]))

    zeros = jnp.zeros((16, buf.shape[1]), buf.dtype)
    return jnp.max(lax.fori_loop(0, buf.shape[0] // 16, step, zeros).astype(jnp.float32))


def lanes(place):
    return pl.ds(pl.multiple_of(place * 128, 128), 128)


def load_and_turn(acts, at, pieces, buf, left, sems, meanwhile=lambda: None):
    copies = load(pieces, buf, sems)
    meanwhile()
    for first in range(0, len(pieces), 2):
        copies[first].wait()
        copies[first + 1].wait()
        here = slice(first * pieces[0].shape[0], (first + 2) * pieces[0].shape[0])

        def turn_tile(i, _, here=here):
            tile = at[0] * 8 + i if acts else lax.rem(i + at[2], NZ) * 4 + at[0]
            left[lanes(i), here] = jnp.transpose(buf[here, lanes(tile)])
            return 0

        lax.fori_loop(0, 8, turn_tile, 0)


def target_of(role, at):
    ahead = jnp.where(at[3] == 0, 1, 3)
    away = jnp.where(role == 0, 2, jnp.where(role == 3, 0, ahead))
    return lax.rem(at[1] + away, 4)


def half_of(role, at):
    return jnp.where(role == 1, 1 - at[3], at[3])


def unit_tile(role, i, at):
    z = lax.rem(half_of(role, at) * 4 + i + at[2], NZ)
    return z * 4 + target_of(role, at)


def products(acts, at, buf, left, store):
    role, first = pl.program_id(0) // 2, lax.rem(pl.program_id(0), 2) * 2
    if acts:
        columns = jnp.concatenate([buf[:, lanes(unit_tile(role, first + i, at))] for i in range(2)], axis=1)

        def one_half(half, _):
            rows = pl.ds(pl.multiple_of(half * 512, 512), 512)
            out = jnp.dot(left[rows, :], columns, preferred_element_type=jnp.float32)
            for i in range(2):
                store(i, rows, out[:, i * 128 : (i + 1) * 128])
            return 0

        lax.fori_loop(0, 2, one_half, 0)
        return
    rows = left[pl.ds(pl.multiple_of(half_of(role, at) * 512 + first * 128, 256), 256), :]

    def one_core(core, _):
        start = pl.multiple_of((2 * target_of(role, at) + core) * 512, 512)
        out = jnp.dot(rows, buf[:, pl.ds(start, 512)], preferred_element_type=jnp.float32)
        for i in range(2):
            for part in range(4):
                store(i, lanes(core * 4 + part), out[i * 128 : (i + 1) * 128, part * 128 : (part + 1) * 128])
        return 0

    lax.fori_loop(0, 2, one_core, 0)


def early_kernel(at, *refs, count, acts):
    pieces, (out, peak, buf, left, sems) = refs[:count], refs[count:]

    @pl.when(pl.program_id(0) == 0)
    def _():
        load_and_turn(acts, at, pieces, buf, left, sems)
        peak[...] = jnp.full(peak.shape, largest(buf), jnp.float32)

    def store(i, rows, value):
        out[0, i, rows] = value

    products(acts, at, buf, left, store)


def late_kernel(at, early_peak, early, *refs, count, acts, tokens):
    pieces, (sent, kept, buf, left, exponent, sums, sums_sems, sems) = refs[:count], refs[count:]
    step = pl.program_id(0)

    def fetch(i):
        part = early.at[i // 2, pl.ds(lax.rem(i, 2) * 2, 2)]
        return pltpu.make_async_copy(part, sums.at[i], sums_sems.at[i])

    @pl.when(step == 0)
    def _():
        def fetch_all():
            for i in range(8):
                fetch(jnp.int32(i)).start()

        load_and_turn(acts, at, pieces, buf, left, sems, fetch_all)
        peak = jnp.maximum(early_peak[0:1, :], largest(buf))
        bound = tokens * jnp.maximum(peak * peak, 1e-35)
        exponent[...] = jnp.broadcast_to(jnp.floor(jnp.log2(30000.0 / bound)), exponent.shape)

    fetch(step).wait()

    def store(i, rows, value):
        value = sums[step, i, rows] + value

        @pl.when(step < 4)
        def _():
            sent[0, i, rows] = value * jnp.exp2(exponent[0:1, :])

        @pl.when(step >= 4)
        def _():
            kept[0, i, rows] = value

    products(acts, at, buf, left, store)
    for i in range(2):
        sent[0, i, 1024:1040] = exponent[...]
        kept[0, i, 1024:1040] = exponent[...]


def halves(step):
    return step // 2, lax.rem(step, 2), 0, 0


def product(acts, at, pieces, early=(), tokens=None):
    count, rows, width = len(pieces), sum(p.shape[0] for p in pieces), pieces[0].shape[1]
    peak_spec = pl.BlockSpec((8, 128), lambda i, at: (0, 0))
    peak_shape = jax.ShapeDtypeStruct((8, 128), jnp.float32)
    spec = pl.BlockSpec((1, 2, 1024, 128), lambda i, at: halves(i))
    scratch = [
        pltpu.VMEM((rows, width), jnp.bfloat16),
        pltpu.VMEM((1024, rows), jnp.bfloat16),
    ]
    if early:
        kernel = functools.partial(late_kernel, tokens=tokens)
        before = [peak_spec, pl.BlockSpec(memory_space=pltpu.HBM)]
        out_specs = [
            pl.BlockSpec((1, 2, 1040, 128), lambda i, at: halves(jnp.minimum(i, 3))),
            pl.BlockSpec((1, 2, 1040, 128), lambda i, at: halves(jnp.maximum(i - 4, 0))),
        ]
        out_shape = [jax.ShapeDtypeStruct((2, 4, 1040, 128), jnp.float32)] * 2
        scratch += [
            pltpu.VMEM((16, 128), jnp.float32),
            pltpu.VMEM((8, 2, 1024, 128), jnp.float32),
            pltpu.SemaphoreType.DMA((8,)),
        ]
        cost = pl.CostEstimate(
            flops=2 * rows * 1024 * 2048, bytes_accessed=2 * rows * width + 2 * 2048 * 4096, transcendentals=0
        )
    else:
        kernel, before = early_kernel, []
        out_specs = [spec, peak_spec]
        out_shape = [pltpu.HBM((4, 4, 1024, 128), jnp.float32), peak_shape]
        cost = pl.CostEstimate(flops=1, bytes_accessed=1, transcendentals=0)
    return pl.pallas_call(
        functools.partial(kernel, count=count, acts=acts),
        grid_spec=pltpu.PrefetchScalarGridSpec(
            num_scalar_prefetch=1,
            grid=(8,),
            in_specs=before + [pl.BlockSpec(memory_space=pltpu.HBM)] * count,
            out_specs=out_specs,
            scratch_shapes=scratch + [pltpu.SemaphoreType.DMA((count,))],
        ),
        out_shape=out_shape,
        compiler_params=pltpu.CompilerParams(vmem_limit_bytes=VMEM_BYTES),
        cost_estimate=cost,
    )(at, *early[:1], *[pltpu.with_memory_space_constraint(p, pltpu.HBM) for p in (*early[1:], *pieces)])


def gather_line(rows, axis):
    other = send(rows, k=1)
    first = send(rows, fan=axis)
    second = send(other, fan=axis)
    far = send(first, fan=axis)
    return [rows, other, first, send(first, k=1)], [second, far]


def both_cores(pieces):
    return pieces + [send(piece, k=1) for piece in pieces]


def exponent_of(rows):
    return rows[:, -1:].astype(jnp.float32)


def opened(rows):
    return rows[:, :-16].astype(jnp.float32) * jnp.exp2(-exponent_of(rows))


def relayed(kept, relay, exponent_rows):
    both = jnp.minimum(exponent_of(kept), exponent_of(relay)) - 1.0
    total = (kept + relay.astype(jnp.float32) * jnp.exp2(-exponent_of(relay))) * jnp.exp2(both)
    return jnp.where(exponent_rows, both, total).astype(jnp.float16)


def finish_line(own, plain, last, core, factor):
    def columns(value, core):
        return lax.dynamic_slice_in_dim(value, core * 512, 512, 1)

    plain = opened(plain)
    other_own, other_plain = send(jnp.stack([columns(own, 1 - core), columns(plain, 1 - core)]), k=1)
    other_last = send(jnp.concatenate([columns(last, 1 - core), last[:, -16:]], axis=1), k=1)
    this_half = (columns(own, core) + other_plain + columns(opened(last), core)) * factor
    other_half = (columns(plain, core) + other_own + opened(other_last)) * factor
    return jnp.where(core == 0, this_half, other_half), jnp.where(core == 0, other_half, this_half)


def reduce_z(low, high):
    up, down = send(high[0, :256], z=1), send(high[0, 256:], z=-1)
    up = send(jnp.concatenate([low[3, :256] + up, low[3, 256:]], axis=0), z=1)
    down = send(jnp.concatenate([high[1, :256], high[1, 256:] + down], axis=0), z=-1)
    up, down = send(low[2] + up, z=1), send(high[2] + down, z=-1)
    up, down = send(low[1] + up, z=1), send(high[3] + down, z=-1)
    return low[0] + up + down


def body(acts, grads, lengths, assign):
    n_dp = lax.axis_size("dp")
    n_tile = lax.axis_size("tile")
    slot_count, block_len, feat_width = acts.shape
    dp, tile = lax.axis_index("dp"), lax.axis_index("tile")
    my_x, my_k = dp // NK, dp % NK
    my_z, my_y = tile // NY, tile % NY
    positions = jnp.arange(block_len, dtype=jnp.int32)
    live = (positions[:, None] < jnp.pad(lengths, (0, 16 - slot_count))[None, :])[:, :, None]
    rows_a, rows_g = token_rows(acts, live), token_rows(grads, live)
    early_a, late_a = gather_line(rows_a, "x")
    early_g, late_g = gather_line(rows_g, "y")

    scores = block_scores(rows_a, rows_g, block_len)[:slot_count]
    places = jnp.arange(n_dp * KEEP, dtype=jnp.int32)
    placed = jnp.sum(jnp.where(assign[:, None] == places[None, :], scores[:, None], 0.0), axis=0)
    at_a = jnp.stack([my_x, my_y, my_z, my_k])
    at_g = jnp.stack([my_y, my_x, my_z, my_k])
    sum_a, sum_g = product(True, at_a, early_a), product(False, at_g, early_g)
    sum_a, sum_g, placed = lax.optimization_barrier((sum_a, sum_g, placed))
    placed = lax.all_to_all(placed.reshape(n_dp, KEEP), "dp", split_axis=0, concat_axis=0, tiled=True)
    block_norms = jnp.sum(placed, axis=0)
    late_a, late_g, sum_a, sum_g, block_norms = lax.optimization_barrier(
        (late_a, late_g, sum_a, sum_g, block_norms)
    )
    late_a, late_g = both_cores(late_a), both_cores(late_g)
    tokens = n_dp * slot_count * block_len
    sent_a, kept_a = product(True, at_a, late_a, sum_a[::-1], tokens)
    relay_a = sent_a[0].astype(jnp.float16)
    relay_a, sent_a, kept_a, late_g, sum_g = lax.optimization_barrier((relay_a, sent_a, kept_a, late_g, sum_g))
    sent_g, kept_g = product(False, at_g, late_g, sum_g[::-1], tokens)
    row = jnp.arange(1040, dtype=jnp.int32)[None, :, None]

    def send_on(relay, sent, kept, exponent_rows, axis):
        last = relayed(kept[0], send(relay, fan=axis), exponent_rows)
        last, sent = lax.optimization_barrier((last, sent))
        return send(last, fan=axis), send(sent[1].astype(jnp.float16), fan=axis)

    last_a, plain_a = send_on(relay_a, sent_a, kept_a, row >= 1024, "y")
    last_g, plain_g = send_on(sent_g[0].astype(jnp.float16), sent_g, kept_g, row // 16 == 64, "x")
    factor = 1.0 / (n_dp * n_tile * KEEP * block_len)
    act_factor = jnp.transpose(reduce_z(*finish_line(kept_a[1], plain_a, last_a, my_k, factor)))
    total_g = reduce_z(*finish_line(kept_g[1], plain_g, last_g, my_k, factor))
    grad_factor = jnp.concatenate([total_g[at : at + 128] for at in range(0, 512, 128)], axis=1)
    return (act_factor, grad_factor, block_norms)


def solution(mesh):
    in_specs = (
        P(("dp", "tile"), None, None),
        P(("dp", "tile"), None, None),
        P(("dp", "tile")),
        P(("dp", "tile")),
    )
    out_specs = (P("tile", "dp"), P("tile", "dp"), P(("dp", "tile")))
    return jax.shard_map(body, mesh=mesh, in_specs=in_specs, out_specs=out_specs, check_vma=False)
```

```python
import functools

import jax
import jax.numpy as jnp
from jax import lax
from jax.experimental import pallas as pl
from jax.experimental.pallas import tpu as pltpu
from jax.sharding import PartitionSpec as P

KEEP = 12
NX, NK, NZ, NY = 4, 2, 8, 4
AXES = ("dp", "tile")
VMEM_BYTES = 24 * 1024 * 1024


def route(x=0, k=0, z=0, y=0, fan=None):
    pairs = []
    for sx in range(NX):
        for sk in range(NK):
            for sz in range(NZ):
                for sy in range(NY):
                    step = 1 - 2 * sk
                    tx = (sx + x + step * (fan == "x")) % NX
                    ty = (sy + y + step * (fan == "y")) % NY
                    tk, tz = (sk + k) % NK, (sz + z) % NZ
                    source = ((sx * NK + sk) * NZ + sz) * NY + sy
                    pairs.append((source, ((tx * NK + tk) * NZ + tz) * NY + ty))
    return pairs


def send(value, **shift):
    return lax.ppermute(value, AXES, route(**shift))


def token_rows(tokens, live):
    slots, count, width = tokens.shape
    by_position = jnp.pad(jnp.transpose(tokens, (1, 0, 2)), ((0, 0), (0, 16 - slots), (0, 0)))
    return jnp.where(live, by_position, 0).reshape(count * 16, width)


def block_scores(rows_a, rows_g, count):
    def gram(rows):
        return lax.dot_general(
            rows, rows, (((1,), (1,)), ((), ())), preferred_element_type=jnp.float32
        )

    slot = jnp.arange(rows_a.shape[0], dtype=jnp.int32) % 16
    same = slot[:, None] == slot[None, :]
    per_row = jnp.sum(jnp.where(same, gram(rows_a) * gram(rows_g), 0.0), axis=1)
    width = rows_a.shape[1]
    return jnp.sum(per_row.reshape(count, 16), axis=0) * (1.0 / (width * width * count))


def load(pieces, buf, sems):
    copies, start = [], 0
    for i, piece in enumerate(pieces):
        copies.append(pltpu.make_async_copy(piece, buf.at[pl.ds(start, piece.shape[0])], sems.at[i]))
        copies[-1].start()
        start += piece.shape[0]
    return copies


def largest(buf):
    def step(i, so_far):
        return jnp.maximum(so_far, jnp.abs(buf[pl.ds(pl.multiple_of(i * 16, 16), 16), :]))

    zeros = jnp.zeros((16, buf.shape[1]), buf.dtype)
    return jnp.max(lax.fori_loop(0, buf.shape[0] // 16, step, zeros).astype(jnp.float32))


def lanes(place):
    return pl.ds(pl.multiple_of(place * 128, 128), 128)


def load_and_turn(acts, at, pieces, buf, left, sems, meanwhile=lambda: None):
    copies = load(pieces, buf, sems)
    for first in range(0, len(pieces), 2):
        copies[first].wait()
        copies[first + 1].wait()
        if first + 2 == len(pieces):
            meanwhile()
        here = slice(first * pieces[0].shape[0], (first + 2) * pieces[0].shape[0])
        if acts:
            left[:, here] = jnp.transpose(buf[here, pl.ds(pl.multiple_of(at[0] * 1024, 1024), 1024)])
        else:
            for z in range(NZ):
                tile = lanes(lax.rem(z + at[2], NZ) * 4 + at[0])
                left[z * 128 : (z + 1) * 128, here] = jnp.transpose(buf[here, tile])


def target_of(role, at):
    ahead = jnp.where(at[3] == 0, 1, 3)
    away = jnp.where(role == 0, 2, jnp.where(role == 3, 0, ahead))
    return lax.rem(at[1] + away, 4)


def half_of(role, at):
    return jnp.where(role == 1, 1 - at[3], at[3])


def unit_tile(role, i, at):
    z = lax.rem(half_of(role, at) * 4 + i + at[2], NZ)
    return z * 4 + target_of(role, at)


def products(acts, at, buf, left, store):
    role, first = pl.program_id(0) // 2, lax.rem(pl.program_id(0), 2) * 2
    if acts:
        columns = jnp.concatenate([buf[:, lanes(unit_tile(role, first + i, at))] for i in range(2)], axis=1)
        out = jnp.dot(left[...], columns, preferred_element_type=jnp.float32)
        for i in range(2):
            store(i, slice(0, 1024), out[:, i * 128 : (i + 1) * 128])
        return
    rows = left[pl.ds(pl.multiple_of(half_of(role, at) * 512 + first * 128, 256), 256), :]
    for core in range(2):
        start = pl.multiple_of((2 * target_of(role, at) + core) * 512, 512)
        out = jnp.dot(rows, buf[:, pl.ds(start, 512)], preferred_element_type=jnp.float32)
        for i in range(2):
            for part in range(4):
                tile = out[i * 128 : (i + 1) * 128, part * 128 : (part + 1) * 128]
                store(i, slice((core * 4 + part) * 128, (core * 4 + part + 1) * 128), tile)


def early_kernel(at, *refs, count, acts):
    pieces, (out, peak, buf, left, sems) = refs[:count], refs[count:]

    @pl.when(pl.program_id(0) == 0)
    def _():
        load_and_turn(acts, at, pieces, buf, left, sems)
        peak[...] = jnp.full(peak.shape, largest(buf), jnp.float32)

    def store(i, rows, value):
        out[0, i, rows] = value

    products(acts, at, buf, left, store)


def late_kernel(at, early_peak, early, *refs, count, acts, tokens):
    pieces, (sent, kept, buf, left, exponent, sums, sums_sems, sems) = refs[:count], refs[count:]
    step = pl.program_id(0)

    def fetch(i):
        part = early.at[i // 2, pl.ds(lax.rem(i, 2) * 2, 2)]
        return pltpu.make_async_copy(part, sums.at[i], sums_sems.at[i])

    @pl.when(step == 0)
    def _():
        def fetch_all():
            for i in range(8):
                fetch(jnp.int32(i)).start()

        load_and_turn(acts, at, pieces, buf, left, sems, fetch_all)
        peak = jnp.maximum(early_peak[0:1, :], largest(buf))
        bound = tokens * jnp.maximum(peak * peak, 1e-35)
        exponent[...] = jnp.broadcast_to(jnp.floor(jnp.log2(30000.0 / bound)), exponent.shape)

    fetch(step).wait()

    def into(out, scale):
        def store(i, rows, value):
            out[0, i, rows] = (sums[step, i, rows] + value) * scale

        products(acts, at, buf, left, store)
        for i in range(2):
            out[0, i, 1024:1040] = exponent[...]

    @pl.when(pl.program_id(0) < 4)
    def _():
        into(sent, jnp.exp2(exponent[0:1, :]))

    @pl.when(pl.program_id(0) >= 4)
    def _():
        into(kept, 1.0)


def halves(step):
    return step // 2, lax.rem(step, 2), 0, 0


def product(acts, at, pieces, early=(), tokens=None):
    count, rows, width = len(pieces), sum(p.shape[0] for p in pieces), pieces[0].shape[1]
    peak_spec = pl.BlockSpec((8, 128), lambda i, at: (0, 0))
    peak_shape = jax.ShapeDtypeStruct((8, 128), jnp.float32)
    spec = pl.BlockSpec((1, 2, 1024, 128), lambda i, at: halves(i))
    scratch = [
        pltpu.VMEM((rows, width), jnp.bfloat16),
        pltpu.VMEM((1024, rows), jnp.bfloat16),
    ]
    if early:
        kernel = functools.partial(late_kernel, tokens=tokens)
        before = [peak_spec, pl.BlockSpec(memory_space=pltpu.HBM)]
        out_specs = [
            pl.BlockSpec((1, 2, 1040, 128), lambda i, at: halves(jnp.minimum(i, 3))),
            pl.BlockSpec((1, 2, 1040, 128), lambda i, at: halves(jnp.maximum(i - 4, 0))),
        ]
        out_shape = [jax.ShapeDtypeStruct((2, 4, 1040, 128), jnp.float32)] * 2
        scratch += [
            pltpu.VMEM((16, 128), jnp.float32),
            pltpu.VMEM((8, 2, 1024, 128), jnp.float32),
            pltpu.SemaphoreType.DMA((8,)),
        ]
        cost = pl.CostEstimate(
            flops=2 * rows * 1024 * 2048, bytes_accessed=2 * rows * width + 2 * 2048 * 4096, transcendentals=0
        )
    else:
        kernel, before = early_kernel, []
        out_specs = [spec, peak_spec]
        out_shape = [pltpu.HBM((4, 4, 1024, 128), jnp.float32), peak_shape]
        cost = pl.CostEstimate(flops=1, bytes_accessed=1, transcendentals=0)
    return pl.pallas_call(
        functools.partial(kernel, count=count, acts=acts),
        grid_spec=pltpu.PrefetchScalarGridSpec(
            num_scalar_prefetch=1,
            grid=(8,),
            in_specs=before + [pl.BlockSpec(memory_space=pltpu.HBM)] * count,
            out_specs=out_specs,
            scratch_shapes=scratch + [pltpu.SemaphoreType.DMA((count,))],
        ),
        out_shape=out_shape,
        compiler_params=pltpu.CompilerParams(vmem_limit_bytes=VMEM_BYTES),
        cost_estimate=cost,
    )(at, *early[:1], *[pltpu.with_memory_space_constraint(p, pltpu.HBM) for p in (*early[1:], *pieces)])


def gather_line(rows, axis):
    other = send(rows, k=1)
    first = send(rows, fan=axis)
    second = send(other, fan=axis)
    far = send(first, fan=axis)
    return [rows, other, first, send(first, k=1)], [second, far]


def both_cores(pieces):
    return pieces + [send(piece, k=1) for piece in pieces]


def exponent_of(rows):
    return rows[:, -1:].astype(jnp.float32)


def opened(rows):
    return rows[:, :-16].astype(jnp.float32) * jnp.exp2(-exponent_of(rows))


def relayed(kept, relay, exponent_rows):
    both = jnp.minimum(exponent_of(kept), exponent_of(relay)) - 1.0
    total = (kept + relay.astype(jnp.float32) * jnp.exp2(-exponent_of(relay))) * jnp.exp2(both)
    return jnp.where(exponent_rows, both, total).astype(jnp.float16)


def finish_line(own, plain, last, core, factor):
    def columns(value, core):
        return lax.dynamic_slice_in_dim(value, core * 512, 512, 1)

    plain = opened(plain)
    other_own, other_plain = send(jnp.stack([columns(own, 1 - core), columns(plain, 1 - core)]), k=1)
    other_last = send(jnp.concatenate([columns(last, 1 - core), last[:, -16:]], axis=1), k=1)
    this_half = (columns(own, core) + other_plain + columns(opened(last), core)) * factor
    other_half = (columns(plain, core) + other_own + opened(other_last)) * factor
    return jnp.where(core == 0, this_half, other_half), jnp.where(core == 0, other_half, this_half)


def reduce_z(low, high):
    up, down = send(high[0, :256], z=1), send(high[0, 256:], z=-1)
    up = send(jnp.concatenate([low[3, :256] + up, low[3, 256:]], axis=0), z=1)
    down = send(jnp.concatenate([high[1, :256], high[1, 256:] + down], axis=0), z=-1)
    up, down = send(low[2] + up, z=1), send(high[2] + down, z=-1)
    up, down = send(low[1] + up, z=1), send(high[3] + down, z=-1)
    return low[0] + up + down


def body(acts, grads, lengths, assign):
    n_dp = lax.axis_size("dp")
    n_tile = lax.axis_size("tile")
    slot_count, block_len, feat_width = acts.shape
    dp, tile = lax.axis_index("dp"), lax.axis_index("tile")
    my_x, my_k = dp // NK, dp % NK
    my_z, my_y = tile // NY, tile % NY
    positions = jnp.arange(block_len, dtype=jnp.int32)
    live = (positions[:, None] < jnp.pad(lengths, (0, 16 - slot_count))[None, :])[:, :, None]
    rows_a, rows_g = token_rows(acts, live), token_rows(grads, live)
    early_a, late_a = gather_line(rows_a, "x")
    early_g, late_g = gather_line(rows_g, "y")

    scores = block_scores(rows_a, rows_g, block_len)[:slot_count]
    places = jnp.arange(n_dp * KEEP, dtype=jnp.int32)
    placed = jnp.sum(jnp.where(assign[:, None] == places[None, :], scores[:, None], 0.0), axis=0)
    at_a = jnp.stack([my_x, my_y, my_z, my_k])
    at_g = jnp.stack([my_y, my_x, my_z, my_k])
    sum_a, sum_g = product(True, at_a, early_a), product(False, at_g, early_g)
    sum_a, sum_g, placed = lax.optimization_barrier((sum_a, sum_g, placed))
    placed = lax.all_to_all(placed.reshape(n_dp, KEEP), "dp", split_axis=0, concat_axis=0, tiled=True)
    block_norms = jnp.sum(placed, axis=0)
    late_a, late_g, sum_a, sum_g, block_norms = lax.optimization_barrier(
        (late_a, late_g, sum_a, sum_g, block_norms)
    )
    late_a, late_g = both_cores(late_a), both_cores(late_g)
    tokens = n_dp * slot_count * block_len
    sent_a, kept_a = product(True, at_a, late_a, sum_a[::-1], tokens)
    relay_a = sent_a[0].astype(jnp.float16)
    relay_a, sent_a, kept_a, late_g, sum_g = lax.optimization_barrier((relay_a, sent_a, kept_a, late_g, sum_g))
    sent_g, kept_g = product(False, at_g, late_g, sum_g[::-1], tokens)
    row = jnp.arange(1040, dtype=jnp.int32)[None, :, None]

    def send_on(relay, sent, kept, exponent_rows, axis):
        last = relayed(kept[0], send(relay, fan=axis), exponent_rows)
        last, sent = lax.optimization_barrier((last, sent))
        return send(last, fan=axis), send(sent[1].astype(jnp.float16), fan=axis)

    last_a, plain_a = send_on(relay_a, sent_a, kept_a, row >= 1024, "y")
    last_g, plain_g = send_on(sent_g[0].astype(jnp.float16), sent_g, kept_g, row // 16 == 64, "x")
    factor = 1.0 / (n_dp * n_tile * KEEP * block_len)
    act_factor = jnp.transpose(reduce_z(*finish_line(kept_a[1], plain_a, last_a, my_k, factor)))
    total_g = reduce_z(*finish_line(kept_g[1], plain_g, last_g, my_k, factor))
    grad_factor = jnp.concatenate([total_g[at : at + 128] for at in range(0, 512, 128)], axis=1)
    return (act_factor, grad_factor, block_norms)


def solution(mesh):
    in_specs = (
        P(("dp", "tile"), None, None),
        P(("dp", "tile"), None, None),
        P(("dp", "tile")),
        P(("dp", "tile")),
    )
    out_specs = (P("tile", "dp"), P("tile", "dp"), P(("dp", "tile")))
    return jax.shard_map(body, mesh=mesh, in_specs=in_specs, out_specs=out_specs, check_vma=False)
```

```python
import functools

import jax
import jax.numpy as jnp
from jax import lax
from jax.experimental import pallas as pl
from jax.experimental.pallas import tpu as pltpu
from jax.sharding import PartitionSpec as P

KEEP = 12
NX, NK, NZ, NY = 4, 2, 8, 4
AXES = ("dp", "tile")
VMEM_BYTES = 24 * 1024 * 1024


def route(x=0, k=0, z=0, y=0, fan=None):
    pairs = []
    for sx in range(NX):
        for sk in range(NK):
            for sz in range(NZ):
                for sy in range(NY):
                    step = 1 - 2 * sk
                    tx = (sx + x + step * (fan == "x")) % NX
                    ty = (sy + y + step * (fan == "y")) % NY
                    tk, tz = (sk + k) % NK, (sz + z) % NZ
                    source = ((sx * NK + sk) * NZ + sz) * NY + sy
                    pairs.append((source, ((tx * NK + tk) * NZ + tz) * NY + ty))
    return pairs


def send(value, **shift):
    return lax.ppermute(value, AXES, route(**shift))


def token_rows(tokens, live):
    slots, count, width = tokens.shape
    by_position = jnp.pad(jnp.transpose(tokens, (1, 0, 2)), ((0, 0), (0, 16 - slots), (0, 0)))
    return jnp.where(live, by_position, 0).reshape(count * 16, width)


def block_scores(rows_a, rows_g, count):
    def gram(rows):
        return lax.dot_general(
            rows, rows, (((1,), (1,)), ((), ())), preferred_element_type=jnp.float32
        )

    slot = jnp.arange(rows_a.shape[0], dtype=jnp.int32) % 16
    same = slot[:, None] == slot[None, :]
    per_row = jnp.sum(jnp.where(same, gram(rows_a) * gram(rows_g), 0.0), axis=1)
    width = rows_a.shape[1]
    return jnp.sum(per_row.reshape(count, 16), axis=0) * (1.0 / (width * width * count))


def load(pieces, buf, sems):
    copies, start = [], 0
    for i, piece in enumerate(pieces):
        copies.append(pltpu.make_async_copy(piece, buf.at[pl.ds(start, piece.shape[0])], sems.at[i]))
        copies[-1].start()
        start += piece.shape[0]
    return copies


def largest(buf):
    def step(i, so_far):
        return jnp.maximum(so_far, jnp.abs(buf[pl.ds(pl.multiple_of(i * 16, 16), 16), :]))

    zeros = jnp.zeros((16, buf.shape[1]), buf.dtype)
    return jnp.max(lax.fori_loop(0, buf.shape[0] // 16, step, zeros).astype(jnp.float32))


def lanes(place):
    return pl.ds(pl.multiple_of(place * 128, 128), 128)


def load_and_turn(acts, at, pieces, buf, left, sems, meanwhile=lambda: None):
    copies = load(pieces, buf, sems)
    for first in range(0, len(pieces), 2):
        copies[first].wait()
        copies[first + 1].wait()
        if first + 2 == len(pieces):
            meanwhile()
        here = slice(first * pieces[0].shape[0], (first + 2) * pieces[0].shape[0])
        if acts:
            left[:, here] = jnp.transpose(buf[here, pl.ds(pl.multiple_of(at[0] * 1024, 1024), 1024)])
        else:
            for z in range(NZ):
                tile = lanes(lax.rem(z + at[2], NZ) * 4 + at[0])
                left[z * 128 : (z + 1) * 128, here] = jnp.transpose(buf[here, tile])


def target_of(role, at):
    ahead = jnp.where(at[3] == 0, 1, 3)
    away = jnp.where(role == 0, 2, jnp.where(role == 3, 0, ahead))
    return lax.rem(at[1] + away, 4)


def half_of(role, at):
    return jnp.where(role == 1, 1 - at[3], at[3])


def unit_tile(role, i, at):
    z = lax.rem(half_of(role, at) * 4 + i + at[2], NZ)
    return z * 4 + target_of(role, at)


def products(acts, at, buf, left, store):
    role, first = pl.program_id(0) // 2, lax.rem(pl.program_id(0), 2) * 2
    if acts:
        columns = jnp.concatenate([buf[:, lanes(unit_tile(role, first + i, at))] for i in range(2)], axis=1)
        out = jnp.dot(left[...], columns, preferred_element_type=jnp.float32)
        for i in range(2):
            store(i, slice(0, 1024), out[:, i * 128 : (i + 1) * 128])
        return
    rows = left[pl.ds(pl.multiple_of(half_of(role, at) * 512 + first * 128, 256), 256), :]
    for core in range(2):
        start = pl.multiple_of((2 * target_of(role, at) + core) * 512, 512)
        out = jnp.dot(rows, buf[:, pl.ds(start, 512)], preferred_element_type=jnp.float32)
        for i in range(2):
            for part in range(4):
                tile = out[i * 128 : (i + 1) * 128, part * 128 : (part + 1) * 128]
                store(i, slice((core * 4 + part) * 128, (core * 4 + part + 1) * 128), tile)


def early_kernel(at, *refs, count, acts):
    pieces, (out, peak, buf, left, sems) = refs[:count], refs[count:]

    @pl.when(pl.program_id(0) == 0)
    def _():
        load_and_turn(acts, at, pieces, buf, left, sems)
        peak[...] = jnp.full(peak.shape, largest(buf), jnp.float32)

    def store(i, rows, value):
        out[0, i, rows] = value

    products(acts, at, buf, left, store)


def late_kernel(at, early_peak, early, *refs, count, acts, tokens):
    pieces, (sent, kept, buf, left, exponent, sums, sums_sems, sems) = refs[:count], refs[count:]
    step = pl.program_id(0)

    def fetch(i):
        part = early.at[i // 2, pl.ds(lax.rem(i, 2) * 2, 2)]
        return pltpu.make_async_copy(part, sums.at[i], sums_sems.at[i])

    @pl.when(step == 0)
    def _():
        def fetch_all():
            for i in range(8):
                fetch(jnp.int32(i)).start()

        load_and_turn(acts, at, pieces, buf, left, sems, fetch_all)
        peak = jnp.maximum(early_peak[0:1, :], largest(buf))
        bound = tokens * jnp.maximum(peak * peak, 1e-35)
        exponent[...] = jnp.broadcast_to(jnp.floor(jnp.log2(30000.0 / bound)), exponent.shape)

    fetch(step).wait()

    def into(out, scale):
        def store(i, rows, value):
            out[0, i, rows] = (sums[step, i, rows] + value) * scale

        products(acts, at, buf, left, store)
        for i in range(2):
            out[0, i, 1024:1040] = exponent[...]

    @pl.when(pl.program_id(0) < 4)
    def _():
        into(sent, jnp.exp2(exponent[0:1, :]))

    @pl.when(pl.program_id(0) >= 4)
    def _():
        into(kept, 1.0)


def halves(step):
    return step // 2, lax.rem(step, 2), 0, 0


def product(acts, at, pieces, early=(), tokens=None):
    count, rows, width = len(pieces), sum(p.shape[0] for p in pieces), pieces[0].shape[1]
    peak_spec = pl.BlockSpec((8, 128), lambda i, at: (0, 0))
    peak_shape = jax.ShapeDtypeStruct((8, 128), jnp.float32)
    spec = pl.BlockSpec((1, 2, 1024, 128), lambda i, at: halves(i))
    scratch = [
        pltpu.VMEM((rows, width), jnp.bfloat16),
        pltpu.VMEM((1024, rows), jnp.bfloat16),
    ]
    if early:
        kernel = functools.partial(late_kernel, tokens=tokens)
        before = [peak_spec, pl.BlockSpec(memory_space=pltpu.HBM)]
        out_specs = [
            pl.BlockSpec((1, 2, 1040, 128), lambda i, at: halves(jnp.minimum(i, 3))),
            pl.BlockSpec((1, 2, 1040, 128), lambda i, at: halves(jnp.maximum(i - 4, 0))),
        ]
        out_shape = [jax.ShapeDtypeStruct((2, 4, 1040, 128), jnp.float32)] * 2
        scratch += [
            pltpu.VMEM((16, 128), jnp.float32),
            pltpu.VMEM((8, 2, 1024, 128), jnp.float32),
            pltpu.SemaphoreType.DMA((8,)),
        ]
        cost = pl.CostEstimate(
            flops=2 * rows * 1024 * 2048, bytes_accessed=2 * rows * width + 2 * 2048 * 4096, transcendentals=0
        )
    else:
        kernel, before = early_kernel, []
        out_specs = [spec, peak_spec]
        out_shape = [pltpu.HBM((4, 4, 1024, 128), jnp.float32), peak_shape]
        cost = pl.CostEstimate(flops=1, bytes_accessed=1, transcendentals=0)
    return pl.pallas_call(
        functools.partial(kernel, count=count, acts=acts),
        grid_spec=pltpu.PrefetchScalarGridSpec(
            num_scalar_prefetch=1,
            grid=(8,),
            in_specs=before + [pl.BlockSpec(memory_space=pltpu.HBM)] * count,
            out_specs=out_specs,
            scratch_shapes=scratch + [pltpu.SemaphoreType.DMA((count,))],
        ),
        out_shape=out_shape,
        compiler_params=pltpu.CompilerParams(vmem_limit_bytes=VMEM_BYTES),
        cost_estimate=cost,
    )(at, *early[:1], *[pltpu.with_memory_space_constraint(p, pltpu.HBM) for p in (*early[1:], *pieces)])


def gather_line(rows, axis):
    other = send(rows, k=1)
    first = send(rows, fan=axis)
    second = send(other, fan=axis)
    far = send(first, fan=axis)
    return [rows, other, first, send(first, k=1)], [second, far]


def both_cores(pieces):
    return pieces + [send(piece, k=1) for piece in pieces]


def exponent_of(rows):
    return rows[:, -1:].astype(jnp.float32)


def opened(rows):
    return rows[:, :-16].astype(jnp.float32) * jnp.exp2(-exponent_of(rows))


def relayed(kept, relay, exponent_rows):
    both = jnp.minimum(exponent_of(kept), exponent_of(relay)) - 1.0
    total = (kept + relay.astype(jnp.float32) * jnp.exp2(-exponent_of(relay))) * jnp.exp2(both)
    return jnp.where(exponent_rows, both, total).astype(jnp.float16)


def finish_line(own, plain, last, core, factor):
    def columns(value, core):
        return lax.dynamic_slice_in_dim(value, core * 512, 512, 1)

    plain = opened(plain)
    other_own, other_plain = send(jnp.stack([columns(own, 1 - core), columns(plain, 1 - core)]), k=1)
    other_last = send(jnp.concatenate([columns(last, 1 - core), last[:, -16:]], axis=1), k=1)
    this_half = (columns(own, core) + other_plain + columns(opened(last), core)) * factor
    other_half = (columns(plain, core) + other_own + opened(other_last)) * factor
    return jnp.where(core == 0, this_half, other_half), jnp.where(core == 0, other_half, this_half)


def reduce_z(low, high):
    up, down = send(high[0, :256], z=1), send(high[0, 256:], z=-1)
    up = send(jnp.concatenate([low[3, :256] + up, low[3, 256:]], axis=0), z=1)
    down = send(jnp.concatenate([high[1, :256], high[1, 256:] + down], axis=0), z=-1)
    up, down = send(low[2] + up, z=1), send(high[2] + down, z=-1)
    up, down = send(low[1] + up, z=1), send(high[3] + down, z=-1)
    return low[0] + up + down


def body(acts, grads, lengths, assign):
    n_dp = lax.axis_size("dp")
    n_tile = lax.axis_size("tile")
    slot_count, block_len, feat_width = acts.shape
    dp, tile = lax.axis_index("dp"), lax.axis_index("tile")
    my_x, my_k = dp // NK, dp % NK
    my_z, my_y = tile // NY, tile % NY
    positions = jnp.arange(block_len, dtype=jnp.int32)
    live = (positions[:, None] < jnp.pad(lengths, (0, 16 - slot_count))[None, :])[:, :, None]
    rows_a, rows_g = token_rows(acts, live), token_rows(grads, live)
    early_a, late_a = gather_line(rows_a, "x")
    early_g, late_g = gather_line(rows_g, "y")

    scores = block_scores(rows_a, rows_g, block_len)[:slot_count]
    places = jnp.arange(n_dp * KEEP, dtype=jnp.int32)
    placed = jnp.sum(jnp.where(assign[:, None] == places[None, :], scores[:, None], 0.0), axis=0)
    at_a = jnp.stack([my_x, my_y, my_z, my_k])
    at_g = jnp.stack([my_y, my_x, my_z, my_k])
    sum_a, sum_g = product(True, at_a, early_a), product(False, at_g, early_g)
    sum_a, sum_g, placed = lax.optimization_barrier((sum_a, sum_g, placed))
    placed = lax.all_to_all(placed.reshape(n_dp, KEEP), "dp", split_axis=0, concat_axis=0, tiled=True)
    block_norms = jnp.sum(placed, axis=0)
    late_a, late_g, sum_a, sum_g, block_norms = lax.optimization_barrier(
        (late_a, late_g, sum_a, sum_g, block_norms)
    )
    late_a, late_g = lax.optimization_barrier((both_cores(late_a), late_g))
    late_g = both_cores(late_g)
    tokens = n_dp * slot_count * block_len
    sent_a, kept_a = product(True, at_a, late_a, sum_a[::-1], tokens)
    relay_a = sent_a[0].astype(jnp.float16)
    relay_a, sent_a, kept_a, late_g, sum_g = lax.optimization_barrier((relay_a, sent_a, kept_a, late_g, sum_g))
    sent_g, kept_g = product(False, at_g, late_g, sum_g[::-1], tokens)
    row = jnp.arange(1040, dtype=jnp.int32)[None, :, None]

    def send_on(relay, sent, kept, exponent_rows, axis):
        last = relayed(kept[0], send(relay, fan=axis), exponent_rows)
        last, sent = lax.optimization_barrier((last, sent))
        return send(last, fan=axis), send(sent[1].astype(jnp.float16), fan=axis)

    last_a, plain_a = send_on(relay_a, sent_a, kept_a, row >= 1024, "y")
    last_g, plain_g = send_on(sent_g[0].astype(jnp.float16), sent_g, kept_g, row // 16 == 64, "x")
    factor = 1.0 / (n_dp * n_tile * KEEP * block_len)
    act_factor = jnp.transpose(reduce_z(*finish_line(kept_a[1], plain_a, last_a, my_k, factor)))
    total_g = reduce_z(*finish_line(kept_g[1], plain_g, last_g, my_k, factor))
    grad_factor = jnp.concatenate([total_g[at : at + 128] for at in range(0, 512, 128)], axis=1)
    return (act_factor, grad_factor, block_norms)


def solution(mesh):
    in_specs = (
        P(("dp", "tile"), None, None),
        P(("dp", "tile"), None, None),
        P(("dp", "tile")),
        P(("dp", "tile")),
    )
    out_specs = (P("tile", "dp"), P("tile", "dp"), P(("dp", "tile")))
    return jax.shard_map(body, mesh=mesh, in_specs=in_specs, out_specs=out_specs, check_vma=False)
```
